256 devices in a mesh: inst: 16 (over z_lo, x, core), tp: 16 (over z_hi, y).
Axes of the slice: x: 4, y: 4, z: 8 (z_hi: 4, z_lo: 2; z = z_hi * 2 + z_lo), core: 2. Of those that a mesh axis runs over, the one named last changes fastest.
Arguments:
- hidden: bfloat16 [256, 2, 8192], P('inst'), may hold values from -6 to 6
- gain: bfloat16 [8192], P('tp'), may hold values from 0.099609375 to 1.8984375
- wqkv: bfloat16 [8192, 5120], P('tp'), may hold values from -0.0625 to 0.0625
- pool: bfloat16 [16, 16, 128, 128, 256], P('inst', 'tp'), may hold values from -240 to 240
- lengths: int32 [16, 4, 4], P('inst'), may hold values from 1 to 3072, as said below
- block_table: int32 [16, 4, 4, 24], P('inst'), may hold values from 0 to 127, as said below
- mig_blocks: int32 [16, 4, 16, 4, 2], P('inst'), may hold values from 0 to 127, as said below
- mig_count: int32 [16, 4, 16, 4], P('inst'), may hold values from 0 to 2, as said below
Outputs:
- attn: bfloat16 [16, 16, 4, 2, 1024], P('inst', 'tp')
The draws below stay inside these ranges and needn't reach their ends.
Inputs may be any that keep to these rules, and one draw needn't show every extreme that they name: `lengths`: some request has 3072 resident tokens. `block_table`: within one instance and part all entries differ, and none of them appears in mig_blocks of that instance and part. `mig_blocks`: entries at or past the count are not lent. `mig_count`: zero from an instance to itself; some request receives 2 blocks from some instance.
All inputs are finite; a program needn't handle non-finite values.
Results may differ from the reference program's by a relative error of at most 0.014.
The reference program's roundings to bfloat16 on the way count: a program that leaves them out, or rounds other values in their place, can miss the bound.
Values may be sent and summed in bfloat16 or wider, within the bound.
No kernel may reach another device: no remote copies, remote signals or barrier semaphores. Data moves between devices by JAX's collectives and lax.ppermute only.
A program may use at most 128 MiB of HBM per device.

```python
import math
import jax
import jax.numpy as jnp
from jax import lax

D = 8192
HEADS = 32
KVH = 4
HD = 128
REQ_DEV = 4
MAXB = 24
MCAP = 2
BLK = 128
QPK = 8
QKV = 5120
PARTS_SIZE = 4
POOL = 128
REQS = 256
N_INST = 16
N_TP = 16


def block_ids(key):
    keys = jax.random.split(key, N_INST * PARTS_SIZE)
    perms = jax.vmap(lambda single: jax.random.permutation(single, POOL))(keys)
    return perms.reshape(N_INST, PARTS_SIZE, POOL).astype(jnp.int32)


def draw_pool(key, part):
    key = jax.random.fold_in(key, 11)
    first_key = jax.random.fold_in(key, 0)
    shape = (N_INST, N_TP, POOL, BLK, 2 * HD)
    base = jnp.clip(jax.random.normal(first_key, shape, jnp.float32), -6.0, 6.0)
    return base.astype(jnp.bfloat16)


def draw_lengths(key, part):
    key = jax.random.fold_in(key, 3)
    drawn = jax.random.randint(key, (N_INST, PARTS_SIZE, REQ_DEV), 1, MAXB * BLK + 1)
    return drawn.at[0, 0, 0].set(MAXB * BLK).astype(jnp.int32)


def draw_block_table(key, part):
    perms = block_ids(key)
    return perms[:, :, :REQ_DEV * MAXB].reshape(N_INST, PARTS_SIZE, REQ_DEV, MAXB)


def draw_mig_blocks(key, part):
    perms = block_ids(key)
    spare = POOL - REQ_DEV * MAXB
    slots = jnp.arange(N_INST * REQ_DEV * MCAP) % spare + REQ_DEV * MAXB
    return perms[:, :, slots].reshape(N_INST, PARTS_SIZE, N_INST, REQ_DEV, MCAP)


def draw_mig_count(key, part):
    key = jax.random.fold_in(key, 5)
    counts = jax.random.randint(key, (N_INST, PARTS_SIZE, N_INST, REQ_DEV), 0, MCAP + 1)
    itself = jnp.arange(N_INST)[:, None, None, None] == jnp.arange(N_INST)[None, None, :, None]
    counts = jnp.where(itself, 0, counts)
    counts = counts.at[0, :, 1, 0].set(MCAP)
    return counts.astype(jnp.int32)


def shard_levels(own_key, shape, pieces, low, high):
    level, own = 1.0, jax.random.fold_in(own_key, 6)
    for axis_at, shards_of in pieces:
        heights = jnp.exp(jax.random.uniform(jax.random.fold_in(own, axis_at), (shards_of,), jnp.float32, low / len(pieces), high / len(pieces)))
        level = level * jnp.repeat(heights, shape[axis_at] // shards_of).reshape([-1 if axis == axis_at else 1 for axis in range(len(shape))])
    return level


def gaussian(rng, extent, scale, most, cuts=(), kind=jnp.bfloat16):
    values = scale * jax.random.normal(rng, extent, jnp.float32)
    if cuts:
        values = values * shard_levels(rng, extent, cuts, -0.22, 0.18)
    return jnp.clip(values, -most, most).astype(kind)


def setup_inputs(seed: int = 0) -> dict:
    key_of = jax.random.split(jax.random.key(seed), 9)
    return {
        "hidden": gaussian(key_of[0], (REQS, 2, D), 1.0, 6.0, ((0, 16),)),
        "gain": jnp.clip(1.0 + 0.18 * jax.random.normal(key_of[1], (D,), jnp.float32), 0.099609375, 1.8984375).astype(jnp.bfloat16),
        "wqkv": gaussian(key_of[2], (D, QKV), D ** -0.5, 0.0625, ((0, 16),)),
        "pool": draw_pool(jax.random.fold_in(key_of[8], 71), 0),
        "lengths": draw_lengths(jax.random.fold_in(key_of[8], 71), 0),
        "block_table": draw_block_table(jax.random.fold_in(key_of[8], 71), 0),
        "mig_blocks": draw_mig_blocks(jax.random.fold_in(key_of[8], 71), 0),
        "mig_count": draw_mig_count(jax.random.fold_in(key_of[8], 71), 0),
    }


EPSILON = 1e-05
NEGATIVE = -1e+30
ROPE_BASE = 500000.0

def rotate(values, position):
    half_dim = values.shape[-1] // 2
    frequency = jnp.exp(jnp.arange(half_dim, dtype=jnp.float32) * (-2.0 * math.log(ROPE_BASE) / values.shape[-1]))
    angles = position.astype(jnp.float32)[..., None] * frequency
    cosine = jnp.cos(angles)
    sine = jnp.sin(angles)
    first_half = values[..., :half_dim]
    second_half = values[..., half_dim:]
    return jnp.concatenate([first_half * cosine - second_half * sine, second_half * cosine + first_half * sine], axis=-1)

def rounded(values):
    return lax.optimization_barrier(values.astype(jnp.bfloat16)).astype(jnp.float32)

def reference(hidden, gain, wqkv, pool, lengths, block_table, mig_blocks, mig_count):
    hidden_f = hidden.astype(jnp.float32)
    inv_rms = lax.rsqrt(lax.optimization_barrier(jnp.mean(hidden_f * hidden_f, axis=-1, keepdims=True)) + EPSILON)
    normed = (hidden_f * inv_rms * gain.astype(jnp.float32)).astype(jnp.bfloat16)
    qkv = jnp.dot(normed.reshape(-1, D), wqkv, preferred_element_type=jnp.float32)
    qkv = qkv.reshape(N_INST, PARTS_SIZE, REQ_DEV, 2, QKV)
    borrowed = jnp.transpose(lax.optimization_barrier(jnp.sum(mig_count, axis=0)), (1, 0, 2))
    context = lengths + BLK * borrowed
    position = context[..., None] + jnp.arange(2, dtype=jnp.int32)
    queries = qkv[..., :HEADS * HD].reshape(N_INST, PARTS_SIZE, REQ_DEV, 2, KVH, QPK, HD)
    queries = rounded(rotate(queries, position[..., None, None]))
    key_new = qkv[..., HEADS * HD:HEADS * HD + KVH * HD].reshape(N_INST, PARTS_SIZE, REQ_DEV, 2, KVH, HD)
    key_new = rounded(rotate(key_new, position[..., None]))
    value_new = rounded(qkv[..., HEADS * HD + KVH * HD:].reshape(N_INST, PARTS_SIZE, REQ_DEV, 2, KVH, HD))
    pool_split = pool.reshape(N_INST, KVH, PARTS_SIZE, POOL, BLK, 2 * HD)
    part_index = jnp.arange(PARTS_SIZE, dtype=jnp.int32)
    source_index = jnp.arange(N_INST, dtype=jnp.int32)
    causal = jnp.arange(2)[None, :] <= jnp.arange(2)[:, None]
    root = math.sqrt(HD)

    def one_instance(instance):
        resident = pool_split[instance][:, part_index[:, None, None], block_table[instance]]
        resident = resident.reshape(KVH, PARTS_SIZE, REQ_DEV, MAXB * BLK, 2 * HD).astype(jnp.float32)
        lent_ids = mig_blocks[:, :, instance]
        lent = pool_split[source_index[:, None, None, None], :, part_index[None, :, None, None], lent_ids]
        lent = jnp.transpose(lent, (4, 1, 2, 0, 3, 5, 6)).reshape(KVH, PARTS_SIZE, REQ_DEV, N_INST * MCAP * BLK, 2 * HD).astype(jnp.float32)
        valid_res = jnp.arange(MAXB * BLK)[None, None, :] < lengths[instance][:, :, None]
        slot_index = jnp.arange(N_INST * MCAP * BLK) // BLK
        counts = mig_count[:, :, instance][slot_index // MCAP]
        valid_lent = jnp.transpose((slot_index % MCAP)[:, None, None] < counts, (1, 2, 0))
        query_here = queries[instance]
        score_res = jnp.einsum('srpgqd,gsrkd->gsrpqk', query_here, resident[..., :HD]) / root
        score_lent = jnp.einsum('srpgqd,gsrkd->gsrpqk', query_here, lent[..., :HD]) / root
        score_new = jnp.einsum('srpgqd,srngd->gsrpqn', query_here, key_new[instance]) / root
        mask_res = valid_res[None, :, :, None, None, :]
        mask_lent = valid_lent[None, :, :, None, None, :]
        mask_new = causal[None, None, None, :, None, :]
        peak_value = jnp.maximum(lax.optimization_barrier(jnp.max(jnp.where(mask_res, score_res, NEGATIVE), axis=-1)), lax.optimization_barrier(jnp.max(jnp.where(mask_lent, score_lent, NEGATIVE), axis=-1)))
        peak_value = jnp.maximum(peak_value, lax.optimization_barrier(jnp.max(jnp.where(mask_new, score_new, NEGATIVE), axis=-1)))[..., None]
        weight_res = jnp.where(mask_res, jnp.exp(score_res - peak_value), 0.0)
        weight_lent = jnp.where(mask_lent, jnp.exp(score_lent - peak_value), 0.0)
        weight_new = jnp.where(mask_new, jnp.exp(score_new - peak_value), 0.0)
        row_sum = lax.optimization_barrier(jnp.sum(weight_res, -1)) + lax.optimization_barrier(jnp.sum(weight_lent, -1)) + lax.optimization_barrier(jnp.sum(weight_new, -1))
        accum = jnp.einsum('gsrpqk,gsrkd->gsrpqd', rounded(weight_res), resident[..., HD:])
        accum = accum + jnp.einsum('gsrpqk,gsrkd->gsrpqd', rounded(weight_lent), lent[..., HD:])
        accum = accum + jnp.einsum('gsrpqn,srngd->gsrpqd', rounded(weight_new), value_new[instance])
        result = (accum / row_sum[..., None]).astype(jnp.bfloat16)
        return result.reshape(KVH * PARTS_SIZE, REQ_DEV, 2, QPK * HD)
    return lax.map(one_instance, jnp.arange(N_INST, dtype=jnp.int32))
```

```python
import math

import numpy as np
import jax
import jax.numpy as jnp
from jax import lax
from jax.experimental import pallas as pl
from jax.experimental.pallas import tpu as pltpu
from jax.sharding import PartitionSpec as P

HEADS = 32
KVH = 4
HD = 128
QPK = 8
PARTS = 4
REQ = 4
POS = 2
MAXB = 24
MCAP = 2
BLK = 128
POOL = 128
N = 16
ROWS = PARTS * REQ * POS
QROWS = REQ * POS * QPK
SHARE = 512
WIDE = QPK * HD
MSG = 80
ROOT = 1.0 / math.sqrt(HD)
EPSILON = 1e-05
NEGATIVE = -1e30
ROPE_BASE = 500000.0
MIB = 1 << 20
STEPS = 5
TURN = 4
LEVEL = 128.0

M_LEN = 0
M_TABLE = M_LEN + REQ
M_IDS = M_TABLE + REQ * MAXB
M_COUNT = M_IDS + N * REQ * MCAP
M_ALL = M_COUNT + N * REQ

VMEM = pl.BlockSpec(memory_space=pltpu.VMEM)
SMEM = pl.BlockSpec(memory_space=pltpu.SMEM)
ANY = pl.BlockSpec(memory_space=pl.ANY)


def project_kernel(tp_ref, hidden, gain_ref, w, out_ref, hidden_ref, w_ref, normed_ref, hidden_sem, w_sem):
    hidden_copies = [
        pltpu.make_async_copy(hidden.at[a], hidden_ref.at[pl.ds(POS * a, POS), :], hidden_sem.at[a])
        for a in range(PARTS * REQ)
    ]
    for copy in hidden_copies:
        copy.start()
    w_copies = [
        pltpu.make_async_copy(w.at[:, pl.ds(c * WIDE, WIDE)], w_ref.at[:, pl.ds(c * WIDE, WIDE)], w_sem.at[c])
        for c in range(STEPS)
    ]
    for copy in w_copies:
        copy.start()
    for copy in hidden_copies:
        copy.wait()
    rows = hidden_ref[...].astype(jnp.float32)
    inv = lax.rsqrt(jnp.sum(rows * rows, axis=-1, keepdims=True) / rows.shape[1] + EPSILON)
    at = pl.multiple_of(tp_ref[0] * SHARE, SHARE)
    own = hidden_ref[:, pl.ds(at, SHARE)].astype(jnp.float32)
    normed_ref[...] = (own * inv * gain_ref[...].astype(jnp.float32)[None, :]).astype(jnp.bfloat16)
    for c in range(STEPS):
        w_copies[c].wait()
        y = jnp.dot(normed_ref[...], w_ref[:, c * WIDE : (c + 1) * WIDE], preferred_element_type=jnp.float32)
        for u in range(QPK):
            if c < KVH:
                group, chunk = c, u
            else:
                group, chunk = u % KVH, QPK + u // KVH
            for part in range(PARTS):
                out_ref[group * PARTS + part, chunk * 8 : chunk * 8 + 8, :] = y[
                    part * 8 : part * 8 + 8, u * HD : u * HD + HD
                ]


def rope_kernel(meta_ref, got_ref, part_ref, freq_ref, cos_ref, sin_ref):
    part = part_ref[0]
    row = lax.broadcasted_iota(jnp.int32, (8, HD), 0)
    position = jnp.zeros((8, HD), jnp.int32)
    for r in range(REQ):
        lent = got_ref[0, part * REQ + r]
        for j in range(1, N):
            lent = lent + got_ref[j, part * REQ + r]
        context = meta_ref[M_LEN + r] + BLK * lent
        position = jnp.where(row // POS == r, context + row % POS, position)
    angle = position.astype(jnp.float32) * freq_ref[...]
    sine = jnp.sin(angle)
    lane = lax.broadcasted_iota(jnp.int32, (8, HD), 1)
    cos_ref[...] = jnp.cos(angle)
    sin_ref[...] = jnp.where(lane < HD // 2, -sine, sine)


def finish_kernel(cos_ref, sin_ref, total_ref, q_ref, new_ref):
    cosine, sine = cos_ref[...], sin_ref[...]
    for r in range(REQ):
        both = []
        for p in range(POS):
            at = r * POS + p
            x = total_ref[pl.ds(at, QPK, stride=8), :]
            both.append(x * cosine[at : at + 1] + pltpu.roll(x, HD // 2, 1) * sine[at : at + 1])
        both = jnp.concatenate(both, axis=0).astype(jnp.bfloat16)
        for i in range(N):
            q_ref[i, r * 16 : r * 16 + 16, :] = both
    key = total_ref[64:72, :]
    key = key * cosine + pltpu.roll(key, HD // 2, 1) * sine
    new_ref[...] = jnp.concatenate([key, total_ref[72:80, :]], axis=0).astype(jnp.bfloat16)


def dot_t(a, b):
    return lax.dot_general(a, b, (((1,), (1,)), ((), ())), preferred_element_type=jnp.float32)


def stats_tile(tile, r, columns):
    lane = lax.broadcasted_iota(jnp.int32, (16, HD), 1)
    for k, column in enumerate(columns):
        tile = jnp.where(lane == r * 8 + k, column, tile)
    return tile


def resident_kernel(meta_ref, q_ref, new_ref, pool_ref, acc_ref, stat_ref, score_ref):
    new = new_ref[...].astype(jnp.float32)
    pad = jnp.zeros((HD - 8, HD), jnp.float32)
    key_new = jnp.concatenate([new[:8], pad], axis=0).astype(jnp.bfloat16)
    value_new = jnp.concatenate([new[8:], pad], axis=0).astype(jnp.bfloat16)
    lane = lax.broadcasted_iota(jnp.int32, (16, 2 * BLK), 1)
    lane_new = lax.broadcasted_iota(jnp.int32, (16, BLK), 1)
    position = lax.broadcasted_iota(jnp.int32, (16, BLK), 0) // QPK
    tile = jnp.zeros((16, HD), jnp.float32)
    for r in range(REQ):
        query = q_ref[0, r * 16 : r * 16 + 16, :]
        length = meta_ref[M_LEN + r]
        ids = [meta_ref[M_TABLE + r * MAXB + b] for b in range(MAXB)]
        scores = jnp.where(
            (lane_new >= r * POS) & (lane_new <= r * POS + position), dot_t(query, key_new) * ROOT, NEGATIVE
        )
        score_ref[r, :, MAXB * BLK :] = scores
        top = jnp.max(scores, axis=-1, keepdims=True)
        most = jnp.full((16, 2 * BLK), NEGATIVE, jnp.float32)
        for b in range(0, MAXB, 2):
            keys = jnp.concatenate([pool_ref[ids[b], :, :HD], pool_ref[ids[b + 1], :, :HD]], axis=0)
            scores = jnp.where(lane + b * BLK < length, dot_t(query, keys) * ROOT, NEGATIVE)
            score_ref[r, :, b * BLK : (b + 2) * BLK] = scores
            most = jnp.maximum(most, scores)
        top = jnp.maximum(top, jnp.max(most, axis=-1, keepdims=True))
        weights = jnp.exp(score_ref[r, :, MAXB * BLK :] - top)
        row_sum = jnp.sum(weights, axis=-1, keepdims=True)
        acc = jnp.dot(weights.astype(jnp.bfloat16), value_new, preferred_element_type=jnp.float32)
        sums = jnp.zeros((16, 2 * BLK), jnp.float32)
        for b in range(0, MAXB, 2):
            weights = jnp.exp(score_ref[r, :, b * BLK : (b + 2) * BLK] - top)
            sums = sums + weights
            values = jnp.concatenate([pool_ref[ids[b], :, HD:], pool_ref[ids[b + 1], :, HD:]], axis=0)
            acc = acc + jnp.dot(weights.astype(jnp.bfloat16), values, preferred_element_type=jnp.float32)
        row_sum = row_sum + jnp.sum(sums, axis=-1, keepdims=True)
        acc_ref[r * 16 : r * 16 + 16, :] = acc
        tile = stats_tile(tile, r, (top, row_sum))
    stat_ref[...] = tile


def rounded(x):
    return x.astype(jnp.bfloat16).astype(jnp.float32)


def lent_kernel(meta_ref, q_ref, pool, out_ref, blocks_ref, score_ref, weight_ref, sem):
    for i in range(N):
        for n in range(i * REQ * MCAP, (i + 1) * REQ * MCAP):
            pltpu.make_async_copy(pool.at[meta_ref[M_IDS + n]], blocks_ref.at[n], sem.at[i]).start()
    lane = lax.broadcasted_iota(jnp.int32, (16, 2 * BLK), 1)

    def pair(n, first):
        return blocks_ref[n * MCAP : (n + 1) * MCAP, :, first : first + HD].reshape(MCAP * BLK, HD)

    for start in range(0, N, TURN):
        group = range(start, start + TURN)
        for i in group:
            here = pl.ds(i * REQ * MCAP, REQ * MCAP)
            pltpu.make_async_copy(pool.at[pl.ds(0, REQ * MCAP)], blocks_ref.at[here], sem.at[i]).wait()
        for i in group:
            for r in range(REQ):
                n = i * REQ + r
                scores = dot_t(q_ref[i, r * 16 : r * 16 + 16, :], pair(n, 0)) * ROOT
                score_ref[n] = jnp.where(lane < meta_ref[M_COUNT + n] * BLK, scores, NEGATIVE)
        for i in group:
            tile = jnp.zeros((16, HD), jnp.float32)
            for r in range(REQ):
                n = i * REQ + r
                scores = score_ref[n]
                top = jnp.max(scores, axis=-1, keepdims=True)
                weights = jnp.where(lane < meta_ref[M_COUNT + n] * BLK, jnp.exp(scores - top), 0.0)
                row_sum = jnp.sum(weights, axis=-1, keepdims=True)
                weight_ref[n] = weights.astype(jnp.bfloat16)
                high = rounded(top)
                middle = rounded(top - high)
                sum_high = rounded(row_sum)
                tile = stats_tile(tile, r, (high, middle, top - high - middle, sum_high, row_sum - sum_high))
            out_ref[i, 64:80, :] = tile.astype(jnp.bfloat16)
        for i in group:
            for r in range(REQ):
                n = i * REQ + r
                acc = jnp.dot(weight_ref[n], pair(n, HD), preferred_element_type=jnp.float32)
                out_ref[i, r * 16 : r * 16 + 16, :] = acc.astype(jnp.bfloat16)


def combine_kernel(recv_ref, acc_ref, stat_ref, out_ref, total_ref):
    stat = stat_ref[...]
    tops, sums = [], []
    for j in range(N):
        tile = recv_ref[j, 64:80, :].astype(jnp.float32)
        tops.append(tile + pltpu.roll(tile, HD - 1, 1) + pltpu.roll(tile, HD - 2, 1))
        sums.append(pltpu.roll(tile, HD - 3, 1) + pltpu.roll(tile, HD - 4, 1))
    peak = stat
    for j in range(N):
        peak = jnp.maximum(peak, tops[j])
    own = jnp.exp(stat - peak)
    row_sum = own * pltpu.roll(stat, HD - 1, 1)
    scales = []
    for j in range(N):
        scale = jnp.exp(tops[j] - peak)
        row_sum = row_sum + scale * sums[j]
        scales.append(scale)
    for r in range(REQ):
        at = slice(r * 16, r * 16 + 16)

        def spread(tile):
            return jnp.broadcast_to(tile[:, r * 8 : r * 8 + 1], (16, HD))

        acc = spread(own) * acc_ref[at, :]
        for j in range(N):
            acc = acc + spread(scales[j]) * recv_ref[j, at, :].astype(jnp.float32)
        total_ref[at, :] = acc / spread(row_sum)
    for h in range(QPK):
        tile = total_ref[pl.ds(h, 8, stride=QPK), :].astype(jnp.bfloat16)
        for r in range(REQ):
            out_ref[0, 0, r, :, h * HD : (h + 1) * HD] = tile[r * POS : (r + 1) * POS]


def local(hidden, gain, wqkv, pool, lengths, block_table, mig_blocks, mig_count):
    tp_index = lax.axis_index("tp")
    part = tp_index % PARTS
    bf16, f32 = jnp.bfloat16, jnp.float32
    shape = jax.ShapeDtypeStruct
    params = pltpu.CompilerParams

    def own(x):
        return lax.dynamic_index_in_dim(x[0], part, 0, keepdims=False).reshape(-1)

    meta = jnp.concatenate([own(lengths), own(block_table), own(mig_blocks), own(mig_count)])
    part_word = part.reshape(1)
    frequency = np.exp(np.arange(HD // 2) * (-2.0 * math.log(ROPE_BASE) / HD)).astype(np.float32)
    frequency = jnp.asarray(np.concatenate([frequency, frequency])[None, :])
    blocks = pool[0, 0]

    partial_value = pl.pallas_call(
        project_kernel,
        in_specs=[SMEM, ANY, VMEM, ANY],
        out_specs=VMEM,
        out_shape=shape((N, MSG, HD), f32),
        scratch_shapes=[
            pltpu.VMEM((ROWS, N * SHARE), bf16),
            pltpu.VMEM((SHARE, STEPS * WIDE), bf16),
            pltpu.VMEM((ROWS, SHARE), bf16),
            pltpu.SemaphoreType.DMA((PARTS * REQ,)),
            pltpu.SemaphoreType.DMA((STEPS,)),
        ],
        compiler_params=params(vmem_limit_bytes=60 * MIB),
        name="project",
    )(tp_index.reshape(1), hidden, gain, wqkv)
    partial_value = (partial_value * LEVEL).astype(jnp.float16)
    partial_value, mig_count = lax.optimization_barrier((partial_value, mig_count))
    summands = lax.all_to_all(partial_value, "tp", split_axis=0, concat_axis=0, tiled=True)
    counts = jnp.transpose(mig_count[0], (1, 0, 2)).reshape(N, PARTS * REQ)
    got = lax.all_to_all(counts, "inst", split_axis=0, concat_axis=0, tiled=True)
    cosine, sine = pl.pallas_call(
        rope_kernel,
        in_specs=[SMEM, SMEM, SMEM, VMEM],
        out_specs=[VMEM, VMEM],
        out_shape=[shape((8, HD), f32), shape((8, HD), f32)],
        compiler_params=params(vmem_limit_bytes=16 * MIB),
        name="rope",
    )(meta, got, part_word, frequency)
    total = jnp.sum(summands.astype(f32), axis=0) * (1.0 / LEVEL)
    queries, new = pl.pallas_call(
        finish_kernel,
        in_specs=[VMEM, VMEM, VMEM],
        out_specs=[VMEM, VMEM],
        out_shape=[shape((N, QROWS, HD), bf16), shape((16, HD), bf16)],
        compiler_params=params(vmem_limit_bytes=16 * MIB),
        name="finish",
    )(cosine, sine, total)
    asked = lax.all_to_all(queries, "inst", split_axis=0, concat_axis=0, tiled=True)
    acc, stat = pl.pallas_call(
        resident_kernel,
        in_specs=[SMEM, VMEM, VMEM, VMEM],
        out_specs=[VMEM, VMEM],
        out_shape=[shape((QROWS, HD), f32), shape((16, HD), f32)],
        scratch_shapes=[pltpu.VMEM((REQ, 16, (MAXB + 1) * BLK), f32)],
        compiler_params=params(vmem_limit_bytes=24 * MIB),
        cost_estimate=pl.CostEstimate(flops=100 * MIB * 8, bytes_accessed=16 * MIB, transcendentals=MIB),
        name="resident",
    )(meta, queries, new, blocks)
    answers = pl.pallas_call(
        lent_kernel,
        in_specs=[SMEM, VMEM, ANY],
        out_specs=VMEM,
        out_shape=shape((N, MSG, HD), bf16),
        scratch_shapes=[
            pltpu.VMEM((N * REQ * MCAP, BLK, 2 * HD), bf16),
            pltpu.VMEM((N * REQ, 16, 2 * BLK), f32),
            pltpu.VMEM((N * REQ, 16, 2 * BLK), bf16),
            pltpu.SemaphoreType.DMA((N,)),
        ],
        compiler_params=params(vmem_limit_bytes=60 * MIB),
        cost_estimate=pl.CostEstimate(flops=100 * MIB * 8, bytes_accessed=16 * MIB, transcendentals=MIB),
        name="lent",
    )(meta, asked, blocks)
    arrived = lax.all_to_all(answers, "inst", split_axis=0, concat_axis=0, tiled=True)
    return pl.pallas_call(
        combine_kernel,
        in_specs=[VMEM, VMEM, VMEM],
        out_specs=VMEM,
        out_shape=shape((1, 1, REQ, POS, WIDE), bf16),
        scratch_shapes=[pltpu.VMEM((QROWS, HD), f32)],
        compiler_params=params(vmem_limit_bytes=16 * MIB),
        name="combine",
    )(arrived, acc, stat)


def solution(mesh):
    placed = (
        P("inst", None, None),
        P("tp"),
        P("tp", None),
        P("inst", "tp", None, None, None),
        P("inst", None, None),
        P("inst", None, None, None),
        P("inst", None, None, None, None),
        P("inst", None, None, None),
    )
    return jax.shard_map(
        local,
        mesh=mesh,
        in_specs=placed,
        out_specs=P("inst", "tp", None, None, None),
        check_vma=False,
    )
```

```python
import math

import numpy as np
import jax
import jax.numpy as jnp
from jax import lax
from jax.experimental import pallas as pl
from jax.experimental.pallas import tpu as pltpu
from jax.sharding import PartitionSpec as P

HEADS = 32
KVH = 4
HD = 128
QPK = 8
PARTS = 4
REQ = 4
POS = 2
MAXB = 24
MCAP = 2
BLK = 128
POOL = 128
N = 16
ROWS = PARTS * REQ * POS
QROWS = REQ * POS * QPK
SHARE = 512
WIDE = QPK * HD
MSG = 80
ASK = 72
ROOT = 1.0 / math.sqrt(HD)
EPSILON = 1e-05
NEGATIVE = -1e30
ROPE_BASE = 500000.0
MIB = 1 << 20
STEPS = 5
TURN = 4
LEVEL = 128.0

FREQUENCY = np.exp(np.arange(HD // 2) * (-2.0 * math.log(ROPE_BASE) / HD)).astype(np.float32)

VMEM = pl.BlockSpec(memory_space=pltpu.VMEM)
SMEM = pl.BlockSpec(memory_space=pltpu.SMEM)
HBM = pl.BlockSpec(memory_space=pltpu.MemorySpace.HBM)


def own_part():
    return lax.axis_index("tp") % PARTS


def project_kernel(hidden, gain, w, out_ref, hidden_ref, gain_ref, w_ref, normed_ref, hidden_sem, w_sem):
    hidden_copies = [
        pltpu.make_async_copy(hidden.at[a], hidden_ref.at[pl.ds(POS * a, POS), :], hidden_sem.at[a])
        for a in range(PARTS * REQ)
    ]
    hidden_copies.append(pltpu.make_async_copy(gain, gain_ref, hidden_sem.at[PARTS * REQ]))
    for copy in hidden_copies:
        copy.start()
    w_copies = [
        pltpu.make_async_copy(w.at[:, pl.ds(c * WIDE, WIDE)], w_ref.at[:, pl.ds(c * WIDE, WIDE)], w_sem.at[c])
        for c in range(STEPS)
    ]
    for copy in w_copies:
        copy.start()
    for copy in hidden_copies:
        copy.wait()
    rows = hidden_ref[...].astype(jnp.float32)
    inv = lax.rsqrt(jnp.sum(rows * rows, axis=-1, keepdims=True) / rows.shape[1] + EPSILON)
    at = pl.multiple_of(lax.axis_index("tp") * SHARE, SHARE)
    own = hidden_ref[:, pl.ds(at, SHARE)].astype(jnp.float32)
    normed_ref[...] = (own * inv * gain_ref[...].astype(jnp.float32)[None, :]).astype(jnp.bfloat16)
    for c in range(STEPS):
        w_copies[c].wait()
        y = LEVEL * jnp.dot(normed_ref[...], w_ref[:, c * WIDE : (c + 1) * WIDE], preferred_element_type=jnp.float32)
        for u in range(QPK):
            if c < KVH:
                group, chunk = c, u
            else:
                group, chunk = u % KVH, QPK + u // KVH
            for part in range(PARTS):
                out_ref[group * PARTS + part, chunk * 8 : chunk * 8 + 8, :] = y[
                    part * 8 : part * 8 + 8, u * HD : u * HD + HD
                ]


def ask_kernel(lengths_ref, count_ref, total_ref, ask_ref, new_ref):
    part = own_part()
    me = lax.axis_index("inst")
    total = total_ref[...] * (1.0 / LEVEL)
    counts = count_ref[0, part]
    row = lax.broadcasted_iota(jnp.int32, (8, N), 0)
    lane = lax.broadcasted_iota(jnp.int32, (8, N), 1)
    terms = jnp.zeros((8, N), jnp.int32)
    for r in range(REQ):
        lent = jnp.broadcast_to(counts[r : r + 1], (8, N)) * BLK
        own = jnp.where(lane == me, lengths_ref[0, part, r] + row % POS, 0)
        terms = jnp.where(row // POS == r, lent + own, terms)
    terms = jnp.concatenate([terms.astype(jnp.float32), jnp.zeros((8, HD - N), jnp.float32)], axis=1)
    new_ref[...] = total[64:80]
    tiles = []
    for h in range(QPK):
        ask_ref[0, h * 8 : h * 8 + 8, :] = total[h * 8 : h * 8 + 8]
    for at in range(REQ * POS):
        tiles.append(ask_ref[0, pl.ds(at, QPK, stride=8), :])
    tiles.append(terms)
    whole = jnp.concatenate(tiles, axis=0)
    for i in range(N // 2):
        ask_ref[i] = whole


def rotated(x, cosine, sine):
    return x * cosine + pltpu.roll(x, HD // 2, 1) * sine


def dot_t(a, b):
    return lax.dot_general(a, b, (((1,), (1,)), ((), ())), preferred_element_type=jnp.float32)


def stats_tile(tile, r, columns):
    lane = lax.broadcasted_iota(jnp.int32, (16, HD), 1)
    for k, column in enumerate(columns):
        tile = jnp.where(lane == r * 8 + k, column, tile)
    return tile


def resident_kernel(lengths_ref, table_ref, q_ref, new_ref, pool_ref, acc_ref, stat_ref, score_ref):
    part = own_part()
    new = new_ref[...].astype(jnp.float32)
    pad = jnp.zeros((HD - 8, HD), jnp.float32)
    key_new = jnp.concatenate([new[:8], pad], axis=0).astype(jnp.bfloat16)
    value_new = jnp.concatenate([new[8:], pad], axis=0).astype(jnp.bfloat16)
    lane = lax.broadcasted_iota(jnp.int32, (16, 2 * BLK), 1)
    lane_new = lax.broadcasted_iota(jnp.int32, (16, BLK), 1)
    position = lax.broadcasted_iota(jnp.int32, (16, BLK), 0) // QPK
    tile = jnp.zeros((16, HD), jnp.float32)
    for r in range(REQ):
        query = q_ref[r * 16 : r * 16 + 16, :]
        length = lengths_ref[0, part, r]
        scores = jnp.where(
            (lane_new >= r * POS) & (lane_new <= r * POS + position), dot_t(query, key_new) * ROOT, NEGATIVE
        )
        score_ref[r, :, MAXB * BLK :] = scores
        top = jnp.max(scores, axis=-1, keepdims=True)
        most = jnp.full((16, 2 * BLK), NEGATIVE, jnp.float32)

        def pair(b, first):
            halves = [pool_ref[table_ref[0, part, r, b + k], :, first : first + HD] for k in range(2)]
            return jnp.concatenate(halves, axis=0)

        for b in range(0, MAXB, 2):
            scores = jnp.where(lane + b * BLK < length, dot_t(query, pair(b, 0)) * ROOT, NEGATIVE)
            score_ref[r, :, b * BLK : (b + 2) * BLK] = scores
            most = jnp.maximum(most, scores)
        top = jnp.maximum(top, jnp.max(most, axis=-1, keepdims=True))
        weights = jnp.exp(score_ref[r, :, MAXB * BLK :] - top)
        row_sum = jnp.sum(weights, axis=-1, keepdims=True)
        acc = jnp.dot(weights.astype(jnp.bfloat16), value_new, preferred_element_type=jnp.float32)
        sums = jnp.zeros((16, 2 * BLK), jnp.float32)
        for b in range(0, MAXB, 2):
            weights = jnp.exp(score_ref[r, :, b * BLK : (b + 2) * BLK] - top)
            sums = sums + weights
            acc = acc + jnp.dot(weights.astype(jnp.bfloat16), pair(b, HD), preferred_element_type=jnp.float32)
        row_sum = row_sum + jnp.sum(sums, axis=-1, keepdims=True)
        acc_ref[r * 16 : r * 16 + 16, :] = acc
        tile = stats_tile(tile, r, (top, row_sum))
    stat_ref[...] = tile


def rounded(x):
    return x.astype(jnp.bfloat16).astype(jnp.float32)


def lent_kernel(
    ids_ref, count_ref, near_ref, far_ref, new_ref, pool_ref, out_ref, own_ref, own_new_ref, q_ref, score_ref, weight_ref
):
    part = own_part()
    me = lax.axis_index("inst")
    lane = lax.broadcasted_iota(jnp.int32, (8, HD), 1)
    frequency = jnp.zeros((8, HD), jnp.float32)
    for m in range(HD // 2):
        frequency = jnp.where(lane % (HD // 2) == m, float(FREQUENCY[m]), frequency)
    positions = near_ref[0, QROWS:ASK, :] + far_ref[0, QROWS:ASK, :]
    for j in range(1, N // 2):
        positions = positions + (near_ref[j, QROWS:ASK, :] + far_ref[j, QROWS:ASK, :])

    def tables(position):
        angle = position * frequency
        sine = jnp.sin(angle)
        return jnp.cos(angle), jnp.where(lane < HD // 2, -sine, sine)

    core = lax.rem(me, 2)
    for i in range(N):
        ask_ref = near_ref if i % 2 == 0 else far_ref
        source = jnp.where(core == 0, i, i ^ 1)
        position = jnp.where(core == 0, positions[:, i : i + 1], positions[:, (i ^ 1) : (i ^ 1) + 1])
        cosine, sine = tables(jnp.broadcast_to(position, (8, HD)))
        for r in range(REQ):
            both = []
            for at in range(r * POS, r * POS + POS):
                x = ask_ref[i // 2, at * QPK : at * QPK + QPK, :]
                both.append(rotated(x, cosine[at : at + 1], sine[at : at + 1]))
            q_ref[source, r * 16 : r * 16 + 16, :] = jnp.concatenate(both, axis=0).astype(jnp.bfloat16)
    own_ref[...] = q_ref[me]
    own = jnp.sum(jnp.where(lane == me, positions, 0.0), axis=-1, keepdims=True)
    cosine, sine = tables(jnp.broadcast_to(own, (8, HD)))
    key = rotated(new_ref[:8], cosine, sine)
    own_new_ref[...] = jnp.concatenate([key, new_ref[8:]], axis=0).astype(jnp.bfloat16)

    lane = lax.broadcasted_iota(jnp.int32, (16, 2 * BLK), 1)

    def pair(i, r, first):
        halves = [pool_ref[ids_ref[0, part, r, k, i], :, first : first + HD] for k in range(MCAP)]
        return jnp.concatenate(halves, axis=0)

    for start in range(0, N, TURN):
        group = range(start, start + TURN)
        for i in group:
            for r in range(REQ):
                n = i * REQ + r
                scores = dot_t(q_ref[i, r * 16 : r * 16 + 16, :], pair(i, r, 0)) * ROOT
                score_ref[n] = jnp.where(lane < count_ref[0, part, r, i] * BLK, scores, NEGATIVE)
        for i in group:
            tile = jnp.zeros((16, HD), jnp.float32)
            for r in range(REQ):
                n = i * REQ + r
                scores = score_ref[n]
                top = jnp.max(scores, axis=-1, keepdims=True)
                weights = jnp.where(lane < count_ref[0, part, r, i] * BLK, jnp.exp(scores - top), 0.0)
                row_sum = jnp.sum(weights, axis=-1, keepdims=True)
                weight_ref[n] = weights.astype(jnp.bfloat16)
                high = rounded(top)
                middle = rounded(top - high)
                sum_high = rounded(row_sum)
                tile = stats_tile(tile, r, (high, middle, top - high - middle, sum_high, row_sum - sum_high))
            out_ref[i, 64:80, :] = tile.astype(jnp.bfloat16)
        for i in group:
            for r in range(REQ):
                n = i * REQ + r
                acc = jnp.dot(weight_ref[n], pair(i, r, HD), preferred_element_type=jnp.float32)
                out_ref[i, r * 16 : r * 16 + 16, :] = acc.astype(jnp.bfloat16)


def combine_kernel(recv_ref, acc_ref, stat_ref, out_ref, total_ref):
    stat = stat_ref[...]
    tops, sums = [], []
    for j in range(N):
        tile = recv_ref[j, 64:80, :].astype(jnp.float32)
        tops.append(tile + pltpu.roll(tile, HD - 1, 1) + pltpu.roll(tile, HD - 2, 1))
        sums.append(pltpu.roll(tile, HD - 3, 1) + pltpu.roll(tile, HD - 4, 1))
    peak = stat
    for j in range(N):
        peak = jnp.maximum(peak, tops[j])
    own = jnp.exp(stat - peak)
    row_sum = own * pltpu.roll(stat, HD - 1, 1)
    scales = []
    for j in range(N):
        scale = jnp.exp(tops[j] - peak)
        row_sum = row_sum + scale * sums[j]
        scales.append(scale)
    for r in range(REQ):
        at = slice(r * 16, r * 16 + 16)

        def spread(tile):
            return jnp.broadcast_to(tile[:, r * 8 : r * 8 + 1], (16, HD))

        acc = spread(own) * acc_ref[at, :]
        for j in range(N):
            acc = acc + spread(scales[j]) * recv_ref[j, at, :].astype(jnp.float32)
        total_ref[at, :] = acc / spread(row_sum)
    for h in range(QPK):
        tile = total_ref[pl.ds(h, 8, stride=QPK), :].astype(jnp.bfloat16)
        for r in range(REQ):
            out_ref[0, 0, r, :, h * HD : (h + 1) * HD] = tile[r * POS : (r + 1) * POS]


def local(hidden, gain, wqkv, pool, lengths, block_table, mig_blocks, mig_count):
    bf16, f32 = jnp.bfloat16, jnp.float32
    shape = jax.ShapeDtypeStruct
    params = pltpu.CompilerParams
    ids = jnp.transpose(mig_blocks, (0, 1, 3, 4, 2))
    counts = jnp.transpose(mig_count, (0, 1, 3, 2))
    blocks = pool[0, 0]

    partial_value = pl.pallas_call(
        project_kernel,
        in_specs=[HBM, HBM, HBM],
        out_specs=VMEM,
        out_shape=shape((N, MSG, HD), f32),
        scratch_shapes=[
            pltpu.VMEM((ROWS, N * SHARE), bf16),
            pltpu.VMEM((SHARE,), bf16),
            pltpu.VMEM((SHARE, STEPS * WIDE), bf16),
            pltpu.VMEM((ROWS, SHARE), bf16),
            pltpu.SemaphoreType.DMA((PARTS * REQ + 1,)),
            pltpu.SemaphoreType.DMA((STEPS,)),
        ],
        compiler_params=params(vmem_limit_bytes=60 * MIB),
        name="project",
    )(hidden, gain, wqkv)
    partial_value = partial_value.astype(jnp.float16)
    summands = lax.all_to_all(partial_value, "tp", split_axis=0, concat_axis=0, tiled=True)
    total = jnp.sum(summands.astype(f32), axis=0)
    ask, new = pl.pallas_call(
        ask_kernel,
        in_specs=[SMEM, VMEM, VMEM],
        out_specs=[VMEM, VMEM],
        out_shape=[shape((N // 2, ASK, HD), f32), shape((16, HD), f32)],
        compiler_params=params(vmem_limit_bytes=16 * MIB),
        cost_estimate=pl.CostEstimate(flops=MIB, bytes_accessed=64 * MIB, transcendentals=0),
        name="ask",
    )(lengths, counts, total)
    groups = [[i for i in range(N) if i % 2 == core] for core in range(2)]
    near = lax.all_to_all(ask, "inst", split_axis=0, concat_axis=0, tiled=True, axis_index_groups=groups)
    far = lax.ppermute(near, "inst", [(i, i ^ 1) for i in range(N)])
    answers, queries, new = pl.pallas_call(
        lent_kernel,
        in_specs=[SMEM, SMEM, VMEM, VMEM, VMEM, VMEM],
        out_specs=[VMEM, VMEM, VMEM],
        out_shape=[shape((N, MSG, HD), bf16), shape((QROWS, HD), bf16), shape((16, HD), bf16)],
        scratch_shapes=[
            pltpu.VMEM((N, QROWS, HD), bf16),
            pltpu.VMEM((N * REQ, 16, 2 * BLK), f32),
            pltpu.VMEM((N * REQ, 16, 2 * BLK), bf16),
        ],
        compiler_params=params(vmem_limit_bytes=24 * MIB),
        name="lent",
    )(ids, counts, near, far, new, blocks)
    acc, stat = pl.pallas_call(
        resident_kernel,
        in_specs=[SMEM, SMEM, VMEM, VMEM, VMEM],
        out_specs=[VMEM, VMEM],
        out_shape=[shape((QROWS, HD), f32), shape((16, HD), f32)],
        scratch_shapes=[
            pltpu.VMEM((REQ, 16, (MAXB + 1) * BLK), f32),
        ],
        compiler_params=params(vmem_limit_bytes=24 * MIB),
        cost_estimate=pl.CostEstimate(flops=100 * MIB * 8, bytes_accessed=16 * MIB, transcendentals=MIB),
        name="resident",
    )(lengths, block_table, queries, new, blocks)
    arrived = lax.all_to_all(answers, "inst", split_axis=0, concat_axis=0, tiled=True)
    return pl.pallas_call(
        combine_kernel,
        in_specs=[VMEM, VMEM, VMEM],
        out_specs=VMEM,
        out_shape=shape((1, 1, REQ, POS, WIDE), bf16),
        scratch_shapes=[pltpu.VMEM((QROWS, HD), f32)],
        compiler_params=params(vmem_limit_bytes=16 * MIB),
        name="combine",
    )(arrived, acc, stat)


def solution(mesh):
    placed = (
        P("inst", None, None),
        P("tp"),
        P("tp", None),
        P("inst", "tp", None, None, None),
        P("inst", None, None),
        P("inst", None, None, None),
        P("inst", None, None, None, None),
        P("inst", None, None, None),
    )
    return jax.shard_map(
        local,
        mesh=mesh,
        in_specs=placed,
        out_specs=P("inst", "tp", None, None, None),
        check_vma=False,
    )
```

```python
import math

import numpy as np
import jax
import jax.numpy as jnp
from jax import lax
from jax.experimental import pallas as pl
from jax.experimental.pallas import tpu as pltpu
from jax.sharding import PartitionSpec as P

HEADS = 32
KVH = 4
HD = 128
QPK = 8
PARTS = 4
REQ = 4
POS = 2
MAXB = 24
MCAP = 2
BLK = 128
POOL = 128
N = 16
NEAR = N // 2
ROWS = PARTS * REQ * POS
QROWS = REQ * POS * QPK
SHARE = 512
WIDE = QPK * HD
MSG = 80
ASK = 72
ROOT = 1.0 / math.sqrt(HD)
EPSILON = 1e-05
NEGATIVE = -1e30
ROPE_BASE = 500000.0
MIB = 1 << 20
STEPS = 5
TURN = 2
LEVEL = 128.0

FREQUENCY = np.exp(np.arange(HD // 2) * (-2.0 * math.log(ROPE_BASE) / HD)).astype(np.float32)

VMEM = pl.BlockSpec(memory_space=pltpu.VMEM)
SMEM = pl.BlockSpec(memory_space=pltpu.SMEM)
ANY = pl.BlockSpec(memory_space=pl.ANY)


def own_part():
    return lax.axis_index("tp") % PARTS


def project_kernel(hidden, gain, w, out_ref, hidden_ref, gain_ref, w_ref, normed_ref, hidden_sem, w_sem):
    hidden_copies = [
        pltpu.make_async_copy(hidden.at[a], hidden_ref.at[pl.ds(POS * a, POS), :], hidden_sem.at[a])
        for a in range(PARTS * REQ)
    ]
    hidden_copies.append(pltpu.make_async_copy(gain, gain_ref, hidden_sem.at[PARTS * REQ]))
    for copy in hidden_copies:
        copy.start()
    w_copies = [
        pltpu.make_async_copy(w.at[:, pl.ds(c * WIDE, WIDE)], w_ref.at[:, pl.ds(c * WIDE, WIDE)], w_sem.at[c])
        for c in range(STEPS)
    ]
    for copy in w_copies:
        copy.start()
    for copy in hidden_copies:
        copy.wait()
    rows = hidden_ref[...].astype(jnp.float32)
    inv = lax.rsqrt(jnp.sum(rows * rows, axis=-1, keepdims=True) / rows.shape[1] + EPSILON)
    at = pl.multiple_of(lax.axis_index("tp") * SHARE, SHARE)
    own = hidden_ref[:, pl.ds(at, SHARE)].astype(jnp.float32)
    normed_ref[...] = (own * inv * gain_ref[...].astype(jnp.float32)[None, :]).astype(jnp.bfloat16)
    for c in range(STEPS):
        w_copies[c].wait()
        y = LEVEL * jnp.dot(normed_ref[...], w_ref[:, c * WIDE : (c + 1) * WIDE], preferred_element_type=jnp.float32)
        for u in range(QPK):
            if c < KVH:
                group, chunk = c, u
            else:
                group, chunk = u % KVH, QPK + u // KVH
            for part in range(PARTS):
                out_ref[group * PARTS + part, chunk * 8 : chunk * 8 + 8, :] = y[
                    part * 8 : part * 8 + 8, u * HD : u * HD + HD
                ]


def ask_kernel(lengths_ref, count_ref, other_count_ref, total_ref, ask_ref, new_ref):
    part = own_part()
    me = lax.axis_index("inst")
    total = total_ref[...] * (1.0 / LEVEL)
    counts = count_ref[0, part] + other_count_ref[0, part]
    row = lax.broadcasted_iota(jnp.int32, (8, N), 0)
    lane = lax.broadcasted_iota(jnp.int32, (8, N), 1)
    terms = jnp.zeros((8, N), jnp.int32)
    for r in range(REQ):
        lent = jnp.broadcast_to(counts[r : r + 1], (8, N)) * BLK
        own = jnp.where(lane == me, lengths_ref[0, part, r] + row % POS, 0)
        terms = jnp.where(row // POS == r, lent + own, terms)
    terms = jnp.concatenate([terms.astype(jnp.float32), jnp.zeros((8, HD - N), jnp.float32)], axis=1)
    new_ref[...] = total[64:80]
    tiles = []
    for h in range(QPK):
        ask_ref[0, h * 8 : h * 8 + 8, :] = total[h * 8 : h * 8 + 8]
    for at in range(REQ * POS):
        tiles.append(ask_ref[0, pl.ds(at, QPK, stride=8), :])
    tiles.append(terms)
    whole = jnp.concatenate(tiles, axis=0)
    for i in range(NEAR):
        ask_ref[i] = whole


def rotated(x, cosine, sine):
    return x * cosine + pltpu.roll(x, HD // 2, 1) * sine


def dot_t(a, b):
    return lax.dot_general(a, b, (((1,), (1,)), ((), ())), preferred_element_type=jnp.float32)


def stats_tile(tile, r, columns):
    lane = lax.broadcasted_iota(jnp.int32, (16, HD), 1)
    for k, column in enumerate(columns):
        tile = jnp.where(lane == r * 8 + k, column, tile)
    return tile


def resident_kernel(lengths_ref, table_ref, q_ref, new_ref, pool, acc_ref, stat_ref, score_ref, blocks_ref, sem):
    part = own_part()
    for r in range(REQ):
        for b in range(MAXB):
            pltpu.make_async_copy(pool.at[table_ref[0, part, r, b]], blocks_ref.at[r * MAXB + b], sem.at[r]).start()
    new = new_ref[...].astype(jnp.float32)
    pad = jnp.zeros((HD - 8, HD), jnp.float32)
    key_new = jnp.concatenate([new[:8], pad], axis=0).astype(jnp.bfloat16)
    value_new = jnp.concatenate([new[8:], pad], axis=0).astype(jnp.bfloat16)
    lane = lax.broadcasted_iota(jnp.int32, (16, 2 * BLK), 1)
    lane_new = lax.broadcasted_iota(jnp.int32, (16, BLK), 1)
    position = lax.broadcasted_iota(jnp.int32, (16, BLK), 0) // QPK
    tile = jnp.zeros((16, HD), jnp.float32)
    for r in range(REQ):
        query = q_ref[r * 16 : r * 16 + 16, :]
        length = lengths_ref[0, part, r]
        scores = jnp.where(
            (lane_new >= r * POS) & (lane_new <= r * POS + position), dot_t(query, key_new) * ROOT, NEGATIVE
        )
        score_ref[r, :, MAXB * BLK :] = scores
        top = jnp.max(scores, axis=-1, keepdims=True)
        most = jnp.full((16, 2 * BLK), NEGATIVE, jnp.float32)

        here = pl.ds(r * MAXB, MAXB)
        pltpu.make_async_copy(pool.at[pl.ds(0, MAXB)], blocks_ref.at[here], sem.at[r]).wait()

        def pair(b, first):
            at = r * MAXB + b
            return blocks_ref[at : at + 2, :, first : first + HD].reshape(2 * BLK, HD)

        for b in range(0, MAXB, 2):
            scores = jnp.where(lane + b * BLK < length, dot_t(query, pair(b, 0)) * ROOT, NEGATIVE)
            score_ref[r, :, b * BLK : (b + 2) * BLK] = scores
            most = jnp.maximum(most, scores)
        top = jnp.maximum(top, jnp.max(most, axis=-1, keepdims=True))
        weights = jnp.exp(score_ref[r, :, MAXB * BLK :] - top)
        row_sum = jnp.sum(weights, axis=-1, keepdims=True)
        acc = jnp.dot(weights.astype(jnp.bfloat16), value_new, preferred_element_type=jnp.float32)
        sums = jnp.zeros((16, 2 * BLK), jnp.float32)
        for b in range(0, MAXB, 2):
            weights = jnp.exp(score_ref[r, :, b * BLK : (b + 2) * BLK] - top)
            sums = sums + weights
            acc = acc + jnp.dot(weights.astype(jnp.bfloat16), pair(b, HD), preferred_element_type=jnp.float32)
        row_sum = row_sum + jnp.sum(sums, axis=-1, keepdims=True)
        acc_ref[r * 16 : r * 16 + 16, :] = acc
        tile = stats_tile(tile, r, (top, row_sum))
    stat_ref[...] = tile


def rounded(x):
    return x.astype(jnp.bfloat16).astype(jnp.float32)


def lent_kernel(
    ids_ref,
    count_ref,
    other_ids_ref,
    other_count_ref,
    ask_ref,
    new_ref,
    pool_ref,
    other_pool_ref,
    out_ref,
    own_ref,
    own_new_ref,
    q_ref,
    score_ref,
    weight_ref,
):
    part = own_part()
    me = lax.axis_index("inst")
    core = lax.rem(me, 2)
    sides = ((ids_ref, count_ref, pool_ref), (other_ids_ref, other_count_ref, other_pool_ref))

    lane = lax.broadcasted_iota(jnp.int32, (8, HD), 1)
    low = lane < HD // 2
    frequency = jnp.zeros((8, HD), jnp.float32)
    for m in range(HD // 2):
        frequency = jnp.where(lane % (HD // 2) == m, float(FREQUENCY[m]), frequency)
    positions = ask_ref[0, QROWS:ASK, :]
    for k in range(1, NEAR):
        positions = positions + ask_ref[k, QROWS:ASK, :]

    def position(k):
        return jnp.where(core == 0, positions[:, 2 * k : 2 * k + 1], positions[:, 2 * k + 1 : 2 * k + 2])

    for first in range(NEAR // 2):
        second = first + NEAR // 2
        angle = jnp.where(low, position(first), position(second)) * frequency
        cosine, sine = jnp.cos(angle), jnp.sin(angle)
        cosine_turned, sine_turned = pltpu.roll(cosine, HD // 2, 1), pltpu.roll(sine, HD // 2, 1)
        for k, cos, sin in (
            (first, jnp.where(low, cosine, cosine_turned), jnp.where(low, -sine, sine_turned)),
            (second, jnp.where(low, cosine_turned, cosine), jnp.where(low, -sine_turned, sine)),
        ):
            for r in range(REQ):
                both = []
                for at in range(r * POS, r * POS + POS):
                    x = ask_ref[k, at * QPK : at * QPK + QPK, :]
                    both.append(rotated(x, cos[at : at + 1], sin[at : at + 1]))
                q_ref[k, r * 16 : r * 16 + 16, :] = jnp.concatenate(both, axis=0).astype(jnp.bfloat16)
    own_ref[...] = q_ref[me // 2]
    own = jnp.sum(jnp.where(lane == me, positions, 0.0), axis=-1, keepdims=True)
    angle = own * frequency
    sine = jnp.sin(angle)
    key = rotated(new_ref[:8], jnp.cos(angle), jnp.where(low, -sine, sine))
    own_new_ref[...] = jnp.concatenate([key, new_ref[8:]], axis=0).astype(jnp.bfloat16)

    lane = lax.broadcasted_iota(jnp.int32, (16, 2 * BLK), 1)

    def valid(n, side):
        return lane < sides[side][1][0, part, n % REQ, 2 * (n // REQ) + core] * BLK

    def pair(n, side, first):
        ids, _, pool = sides[side]
        at = 2 * (n // REQ) + core
        halves = [pool[ids[0, part, n % REQ, b, at], :, first : first + HD] for b in range(MCAP)]
        return jnp.concatenate(halves, axis=0)

    for start in range(0, NEAR * REQ, TURN * REQ):
        group = range(start, start + TURN * REQ)
        for n in group:
            query = q_ref[n // REQ, n % REQ * 16 : n % REQ * 16 + 16, :]
            for side in range(2):
                score_ref[n, side] = jnp.where(valid(n, side), dot_t(query, pair(n, side, 0)) * ROOT, NEGATIVE)
        for n in group:
            r = n % REQ
            if r == 0:
                tile = jnp.zeros((16, HD), jnp.float32)
            top = jnp.max(jnp.maximum(score_ref[n, 0], score_ref[n, 1]), axis=-1, keepdims=True)
            row_sum = jnp.zeros((16, 2 * BLK), jnp.float32)
            for side in range(2):
                weights = jnp.where(valid(n, side), jnp.exp(score_ref[n, side] - top), 0.0)
                row_sum = row_sum + weights
                weight_ref[n, side] = weights.astype(jnp.bfloat16)
            row_sum = jnp.sum(row_sum, axis=-1, keepdims=True)
            high = rounded(top)
            middle = rounded(top - high)
            sum_high = rounded(row_sum)
            tile = stats_tile(tile, r, (high, middle, top - high - middle, sum_high, row_sum - sum_high))
            if r == REQ - 1:
                out_ref[n // REQ, 64:80, :] = tile.astype(jnp.bfloat16)
        for n in group:
            acc = jnp.dot(weight_ref[n, 0], pair(n, 0, HD), preferred_element_type=jnp.float32)
            acc = acc + jnp.dot(weight_ref[n, 1], pair(n, 1, HD), preferred_element_type=jnp.float32)
            out_ref[n // REQ, n % REQ * 16 : n % REQ * 16 + 16, :] = acc.astype(jnp.bfloat16)


def combine_kernel(recv_ref, acc_ref, stat_ref, out_ref, total_ref):
    stat = stat_ref[...]
    tops, sums = [], []
    for j in range(NEAR):
        tile = recv_ref[j, 64:80, :].astype(jnp.float32)
        tops.append(tile + pltpu.roll(tile, HD - 1, 1) + pltpu.roll(tile, HD - 2, 1))
        sums.append(pltpu.roll(tile, HD - 3, 1) + pltpu.roll(tile, HD - 4, 1))
    peak = stat
    for j in range(NEAR):
        peak = jnp.maximum(peak, tops[j])
    own = jnp.exp(stat - peak)
    row_sum = own * pltpu.roll(stat, HD - 1, 1)
    scales = []
    for j in range(NEAR):
        scale = jnp.exp(tops[j] - peak)
        row_sum = row_sum + scale * sums[j]
        scales.append(scale)
    for r in range(REQ):
        at = slice(r * 16, r * 16 + 16)

        def spread(tile):
            return jnp.broadcast_to(tile[:, r * 8 : r * 8 + 1], (16, HD))

        acc = spread(own) * acc_ref[at, :]
        for j in range(NEAR):
            acc = acc + spread(scales[j]) * recv_ref[j, at, :].astype(jnp.float32)
        total_ref[at, :] = acc / spread(row_sum)
    for h in range(QPK):
        tile = total_ref[pl.ds(h, 8, stride=QPK), :].astype(jnp.bfloat16)
        for r in range(REQ):
            out_ref[0, 0, r, :, h * HD : (h + 1) * HD] = tile[r * POS : (r + 1) * POS]


def local(hidden, gain, wqkv, pool, lengths, block_table, mig_blocks, mig_count):
    bf16, f32 = jnp.bfloat16, jnp.float32
    shape = jax.ShapeDtypeStruct
    params = pltpu.CompilerParams
    ids = jnp.transpose(mig_blocks, (0, 1, 3, 4, 2))
    counts = jnp.transpose(mig_count, (0, 1, 3, 2))
    blocks = pool[0, 0]
    swap = [(i, i ^ 1) for i in range(N)]
    other_ids = lax.ppermute(ids, "inst", swap)
    other_counts = lax.ppermute(counts, "inst", swap)
    groups = [[i for i in range(N) if i % 2 == core] for core in range(2)]

    partial_value = pl.pallas_call(
        project_kernel,
        in_specs=[ANY, ANY, ANY],
        out_specs=VMEM,
        out_shape=shape((N, MSG, HD), f32),
        scratch_shapes=[
            pltpu.VMEM((ROWS, N * SHARE), bf16),
            pltpu.VMEM((SHARE,), bf16),
            pltpu.VMEM((SHARE, STEPS * WIDE), bf16),
            pltpu.VMEM((ROWS, SHARE), bf16),
            pltpu.SemaphoreType.DMA((PARTS * REQ + 1,)),
            pltpu.SemaphoreType.DMA((STEPS,)),
        ],
        compiler_params=params(vmem_limit_bytes=24 * MIB),
        cost_estimate=pl.CostEstimate(flops=2 * ROWS * SHARE * STEPS * WIDE, bytes_accessed=8 * MIB, transcendentals=ROWS),
        name="project",
    )(*(pltpu.with_memory_space_constraint(x, pltpu.MemorySpace.HBM) for x in (hidden, gain, wqkv)))
    partial_value = partial_value.astype(jnp.float16)
    partial_value, other_ids, other_counts, lent_blocks = lax.optimization_barrier(
        (partial_value, other_ids, other_counts, blocks)
    )
    other_blocks = lax.ppermute(lent_blocks, "inst", swap)
    summands = lax.all_to_all(partial_value, "tp", split_axis=0, concat_axis=0, tiled=True)
    total = jnp.sum(summands.astype(f32), axis=0)
    total, other_blocks = lax.optimization_barrier((total, other_blocks))
    ask, new = pl.pallas_call(
        ask_kernel,
        in_specs=[SMEM, VMEM, VMEM, VMEM],
        out_specs=[VMEM, VMEM],
        out_shape=[shape((NEAR, ASK, HD), f32), shape((16, HD), f32)],
        compiler_params=params(vmem_limit_bytes=16 * MIB),
        name="ask",
    )(lengths, counts, other_counts, total)
    asked = lax.all_to_all(ask, "inst", split_axis=0, concat_axis=0, tiled=True, axis_index_groups=groups)
    answers, queries, new = pl.pallas_call(
        lent_kernel,
        in_specs=[SMEM, SMEM, SMEM, SMEM, VMEM, VMEM, VMEM, VMEM],
        out_specs=[VMEM, VMEM, VMEM],
        out_shape=[shape((NEAR, MSG, HD), bf16), shape((QROWS, HD), bf16), shape((16, HD), bf16)],
        scratch_shapes=[
            pltpu.VMEM((NEAR, QROWS, HD), bf16),
            pltpu.VMEM((NEAR * REQ, 2, 16, 2 * BLK), f32),
            pltpu.VMEM((NEAR * REQ, 2, 16, 2 * BLK), bf16),
        ],
        compiler_params=params(vmem_limit_bytes=24 * MIB),
        name="lent",
    )(ids, counts, other_ids, other_counts, asked, new, blocks, other_blocks)
    acc, stat = pl.pallas_call(
        resident_kernel,
        in_specs=[SMEM, SMEM, VMEM, VMEM, ANY],
        out_specs=[VMEM, VMEM],
        out_shape=[shape((QROWS, HD), f32), shape((16, HD), f32)],
        scratch_shapes=[
            pltpu.VMEM((REQ, 16, (MAXB + 1) * BLK), f32),
            pltpu.VMEM((REQ * MAXB, BLK, 2 * HD), bf16),
            pltpu.SemaphoreType.DMA((REQ,)),
        ],
        compiler_params=params(vmem_limit_bytes=24 * MIB),
        cost_estimate=pl.CostEstimate(flops=100 * MIB * 8, bytes_accessed=16 * MIB, transcendentals=MIB),
        name="resident",
    )(lengths, block_table, queries, new, pltpu.with_memory_space_constraint(blocks, pltpu.MemorySpace.HBM))
    arrived = lax.all_to_all(answers, "inst", split_axis=0, concat_axis=0, tiled=True, axis_index_groups=groups)
    return pl.pallas_call(
        combine_kernel,
        in_specs=[VMEM, VMEM, VMEM],
        out_specs=VMEM,
        out_shape=shape((1, 1, REQ, POS, WIDE), bf16),
        scratch_shapes=[pltpu.VMEM((QROWS, HD), f32)],
        compiler_params=params(vmem_limit_bytes=16 * MIB),
        name="combine",
    )(arrived, acc, stat)


def solution(mesh):
    placed = (
        P("inst", None, None),
        P("tp"),
        P("tp", None),
        P("inst", "tp", None, None, None),
        P("inst", None, None),
        P("inst", None, None, None),
        P("inst", None, None, None, None),
        P("inst", None, None, None),
    )
    return jax.shard_map(
        local,
        mesh=mesh,
        in_specs=placed,
        out_specs=P("inst", "tp", None, None, None),
        check_vma=False,
    )
```

```python
import math

import numpy as np
import jax
import jax.numpy as jnp
from jax import lax
from jax.experimental import pallas as pl
from jax.experimental.pallas import tpu as pltpu
from jax.sharding import PartitionSpec as P

HEADS = 32
KVH = 4
HD = 128
QPK = 8
PARTS = 4
REQ = 4
POS = 2
MAXB = 24
MCAP = 2
BLK = 128
POOL = 128
N = 16
NEAR = N // 2
ROWS = PARTS * REQ * POS
QROWS = REQ * POS * QPK
SHARE = 512
WIDE = QPK * HD
MSG = 80
ASK = 72
ROOT = 1.0 / math.sqrt(HD)
EPSILON = 1e-05
NEGATIVE = -1e30
ROPE_BASE = 500000.0
MIB = 1 << 20
STEPS = 5
FLIGHT = 3
TURN = 4
LEVEL = 128.0

FREQUENCY = np.exp(np.arange(HD // 2) * (-2.0 * math.log(ROPE_BASE) / HD)).astype(np.float32)

VMEM = pl.BlockSpec(memory_space=pltpu.VMEM)
ANY = pl.BlockSpec(memory_space=pl.ANY)


def own_part():
    return lax.axis_index("tp") % PARTS


def project_kernel(hidden, gain, w, out_ref, hidden_ref, gain_ref, w_ref, normed_ref, hidden_sem, w_sem):
    hidden_copies = [
        pltpu.make_async_copy(hidden.at[a], hidden_ref.at[pl.ds(POS * a, POS), :], hidden_sem.at[a])
        for a in range(PARTS * REQ)
    ]
    hidden_copies.append(pltpu.make_async_copy(gain, gain_ref, hidden_sem.at[PARTS * REQ]))
    for copy in hidden_copies:
        copy.start()
    w_copies = [
        pltpu.make_async_copy(w.at[:, pl.ds(c * WIDE, WIDE)], w_ref.at[:, pl.ds(c * WIDE, WIDE)], w_sem.at[c])
        for c in range(STEPS)
    ]
    for copy in w_copies[:FLIGHT]:
        copy.start()
    for copy in hidden_copies:
        copy.wait()
    rows = hidden_ref[...].astype(jnp.float32)
    inv = lax.rsqrt(jnp.sum(rows * rows, axis=-1, keepdims=True) / rows.shape[1] + EPSILON)
    at = pl.multiple_of(lax.axis_index("tp") * SHARE, SHARE)
    own = hidden_ref[:, pl.ds(at, SHARE)].astype(jnp.float32)
    normed_ref[...] = (own * inv * gain_ref[...].astype(jnp.float32)[None, :]).astype(jnp.bfloat16)
    for c in range(STEPS):
        w_copies[c].wait()
        if c + FLIGHT < STEPS:
            w_copies[c + FLIGHT].start()
        y = LEVEL * jnp.dot(normed_ref[...], w_ref[:, c * WIDE : (c + 1) * WIDE], preferred_element_type=jnp.float32)
        for u in range(QPK):
            if c < KVH:
                group, chunk = c, u
            else:
                group, chunk = u % KVH, QPK + u // KVH
            for part in range(PARTS):
                out_ref[group * PARTS + part, chunk * 8 : chunk * 8 + 8, :] = y[
                    part * 8 : part * 8 + 8, u * HD : u * HD + HD
                ]


def ask_kernel(lengths_ref, count_ref, other_count_ref, total_ref, ask_ref, new_ref):
    part = own_part()
    me = lax.axis_index("inst")
    total = total_ref[...] * (1.0 / LEVEL)
    counts = count_ref[0, part] + other_count_ref[0, part]
    lengths = lengths_ref[0, pl.ds(part, 1), :]
    row = lax.broadcasted_iota(jnp.int32, (8, N), 0)
    lane = lax.broadcasted_iota(jnp.int32, (8, N), 1)
    terms = jnp.zeros((8, N), jnp.int32)
    for r in range(REQ):
        lent = jnp.broadcast_to(counts[r : r + 1], (8, N)) * BLK
        own = jnp.where(lane == me, jnp.broadcast_to(lengths[:, r : r + 1], (8, N)) + row % POS, 0)
        terms = jnp.where(row // POS == r, lent + own, terms)
    terms = jnp.concatenate([terms.astype(jnp.float32), jnp.zeros((8, HD - N), jnp.float32)], axis=1)
    new_ref[...] = total[64:80]
    tiles = []
    for h in range(QPK):
        ask_ref[0, h * 8 : h * 8 + 8, :] = total[h * 8 : h * 8 + 8]
    for at in range(REQ * POS):
        tiles.append(ask_ref[0, pl.ds(at, QPK, stride=8), :])
    tiles.append(terms)
    whole = jnp.concatenate(tiles, axis=0)
    for i in range(NEAR):
        ask_ref[i] = whole


def rotated(x, cosine, sine):
    return x * cosine + pltpu.roll(x, HD // 2, 1) * sine


def dot_t(a, b):
    return lax.dot_general(a, b, (((1,), (1,)), ((), ())), preferred_element_type=jnp.float32)


def stats_tile(tile, r, columns):
    lane = lax.broadcasted_iota(jnp.int32, (16, HD), 1)
    for k, column in enumerate(columns):
        tile = jnp.where(lane == r * 8 + k, column, tile)
    return tile


def resident_kernel(
    lengths, table, q_ref, new_ref, pool, acc_ref, stat_ref, score_ref, blocks_ref, lengths_ref, table_ref, sem, int_sem
):
    part = own_part()
    copies = [
        pltpu.make_async_copy(table.at[0, part], table_ref, int_sem.at[0]),
        pltpu.make_async_copy(lengths.at[0], lengths_ref, int_sem.at[1]),
    ]
    for copy in copies:
        copy.start()
    for copy in copies:
        copy.wait()
    for r in range(REQ):
        for b in range(MAXB):
            pltpu.make_async_copy(pool.at[table_ref[r, b]], blocks_ref.at[r * MAXB + b], sem.at[r]).start()
    new = new_ref[...].astype(jnp.float32)
    pad = jnp.zeros((HD - 8, HD), jnp.float32)
    key_new = jnp.concatenate([new[:8], pad], axis=0).astype(jnp.bfloat16)
    value_new = jnp.concatenate([new[8:], pad], axis=0).astype(jnp.bfloat16)
    lane = lax.broadcasted_iota(jnp.int32, (16, 2 * BLK), 1)
    lane_new = lax.broadcasted_iota(jnp.int32, (16, BLK), 1)
    position = lax.broadcasted_iota(jnp.int32, (16, BLK), 0) // QPK
    tile = jnp.zeros((16, HD), jnp.float32)
    for r in range(REQ):
        query = q_ref[r * 16 : r * 16 + 16, :]
        length = lengths_ref[part, r]
        scores = jnp.where(
            (lane_new >= r * POS) & (lane_new <= r * POS + position), dot_t(query, key_new) * ROOT, NEGATIVE
        )
        score_ref[r, :, MAXB * BLK :] = scores
        top = jnp.max(scores, axis=-1, keepdims=True)
        most = jnp.full((16, 2 * BLK), NEGATIVE, jnp.float32)

        here = pl.ds(r * MAXB, MAXB)
        pltpu.make_async_copy(pool.at[pl.ds(0, MAXB)], blocks_ref.at[here], sem.at[r]).wait()

        def pair(b, first):
            at = r * MAXB + b
            return blocks_ref[at : at + 2, :, first : first + HD].reshape(2 * BLK, HD)

        for b in range(0, MAXB, 2):
            scores = jnp.where(lane + b * BLK < length, dot_t(query, pair(b, 0)) * ROOT, NEGATIVE)
            score_ref[r, :, b * BLK : (b + 2) * BLK] = scores
            most = jnp.maximum(most, scores)
        top = jnp.maximum(top, jnp.max(most, axis=-1, keepdims=True))
        weights = jnp.exp(score_ref[r, :, MAXB * BLK :] - top)
        row_sum = jnp.sum(weights, axis=-1, keepdims=True)
        acc = jnp.dot(weights.astype(jnp.bfloat16), value_new, preferred_element_type=jnp.float32)
        sums = jnp.zeros((16, 2 * BLK), jnp.float32)
        for b in range(0, MAXB, 2):
            weights = jnp.exp(score_ref[r, :, b * BLK : (b + 2) * BLK] - top)
            sums = sums + weights
            acc = acc + jnp.dot(weights.astype(jnp.bfloat16), pair(b, HD), preferred_element_type=jnp.float32)
        row_sum = row_sum + jnp.sum(sums, axis=-1, keepdims=True)
        acc_ref[r * 16 : r * 16 + 16, :] = acc
        tile = stats_tile(tile, r, (top, row_sum))
    stat_ref[...] = tile


def rounded(x):
    return x.astype(jnp.bfloat16).astype(jnp.float32)


def lent_kernel(
    ids,
    counts,
    other_ids,
    other_counts,
    ask_ref,
    new_ref,
    pool_ref,
    other_pool_ref,
    out_ref,
    own_ref,
    own_new_ref,
    q_ref,
    score_ref,
    weight_ref,
    ids_ref,
    count_ref,
    sem,
):
    part = own_part()
    copies = [
        pltpu.make_async_copy(whole.at[0, part], table.at[side], sem.at[at, side])
        for at, (table, both) in enumerate(((ids_ref, (ids, other_ids)), (count_ref, (counts, other_counts))))
        for side, whole in enumerate(both)
    ]
    for copy in copies:
        copy.start()
    me = lax.axis_index("inst")
    core = lax.rem(me, 2)
    pools = (pool_ref, other_pool_ref)

    lane = lax.broadcasted_iota(jnp.int32, (8, HD), 1)
    low = lane < HD // 2
    frequency = jnp.zeros((8, HD), jnp.float32)
    for m in range(HD // 2):
        frequency = jnp.where(lane % (HD // 2) == m, float(FREQUENCY[m]), frequency)
    positions = ask_ref[0, QROWS:ASK, :]
    for k in range(1, NEAR):
        positions = positions + ask_ref[k, QROWS:ASK, :]

    def position(k):
        return jnp.where(core == 0, positions[:, 2 * k : 2 * k + 1], positions[:, 2 * k + 1 : 2 * k + 2])

    for first in range(NEAR // 2):
        second = first + NEAR // 2
        angle = jnp.where(low, position(first), position(second)) * frequency
        cosine, sine = jnp.cos(angle), jnp.sin(angle)
        cosine_turned, sine_turned = pltpu.roll(cosine, HD // 2, 1), pltpu.roll(sine, HD // 2, 1)
        for k, cos, sin in (
            (first, jnp.where(low, cosine, cosine_turned), jnp.where(low, -sine, sine_turned)),
            (second, jnp.where(low, cosine_turned, cosine), jnp.where(low, -sine_turned, sine)),
        ):
            for r in range(REQ):
                both = []
                for at in range(r * POS, r * POS + POS):
                    x = ask_ref[k, at * QPK : at * QPK + QPK, :]
                    both.append(rotated(x, cos[at : at + 1], sin[at : at + 1]))
                q_ref[k, r * 16 : r * 16 + 16, :] = jnp.concatenate(both, axis=0).astype(jnp.bfloat16)
    own_ref[...] = q_ref[me // 2]
    own = jnp.sum(jnp.where(lane == me, positions, 0.0), axis=-1, keepdims=True)
    angle = own * frequency
    sine = jnp.sin(angle)
    key = rotated(new_ref[:8], jnp.cos(angle), jnp.where(low, -sine, sine))
    own_new_ref[...] = jnp.concatenate([key, new_ref[8:]], axis=0).astype(jnp.bfloat16)

    for copy in copies:
        copy.wait()
    lane = lax.broadcasted_iota(jnp.int32, (16, 2 * BLK), 1)

    def valid(n, side):
        return lane < count_ref[side, n % REQ, 2 * (n // REQ) + core] * BLK

    def pair(n, side, first):
        at = 2 * (n // REQ) + core
        halves = [pools[side][ids_ref[side, n % REQ, b, at], :, first : first + HD] for b in range(MCAP)]
        return jnp.concatenate(halves, axis=0)

    for start in range(0, NEAR * REQ, TURN * REQ):
        group = range(start, start + TURN * REQ)
        for n in group:
            query = q_ref[n // REQ, n % REQ * 16 : n % REQ * 16 + 16, :]
            for side in range(2):
                score_ref[n, side] = jnp.where(valid(n, side), dot_t(query, pair(n, side, 0)) * ROOT, NEGATIVE)
        for n in group:
            r = n % REQ
            if r == 0:
                tile = jnp.zeros((16, HD), jnp.float32)
            top = jnp.max(jnp.maximum(score_ref[n, 0], score_ref[n, 1]), axis=-1, keepdims=True)
            row_sum = jnp.zeros((16, 2 * BLK), jnp.float32)
            for side in range(2):
                weights = jnp.where(valid(n, side), jnp.exp(score_ref[n, side] - top), 0.0)
                row_sum = row_sum + weights
                weight_ref[n, side] = weights.astype(jnp.bfloat16)
            row_sum = jnp.sum(row_sum, axis=-1, keepdims=True)
            high = rounded(top)
            middle = rounded(top - high)
            sum_high = rounded(row_sum)
            tile = stats_tile(tile, r, (high, middle, top - high - middle, sum_high, row_sum - sum_high))
            if r == REQ - 1:
                out_ref[n // REQ, 64:80, :] = tile.astype(jnp.bfloat16)
        for n in group:
            acc = jnp.dot(weight_ref[n, 0], pair(n, 0, HD), preferred_element_type=jnp.float32)
            acc = acc + jnp.dot(weight_ref[n, 1], pair(n, 1, HD), preferred_element_type=jnp.float32)
            out_ref[n // REQ, n % REQ * 16 : n % REQ * 16 + 16, :] = acc.astype(jnp.bfloat16)


def combine_kernel(recv_ref, acc_ref, stat_ref, out_ref, total_ref):
    stat = stat_ref[...]
    tops, sums = [], []
    for j in range(NEAR):
        tile = recv_ref[j, 64:80, :].astype(jnp.float32)
        tops.append(tile + pltpu.roll(tile, HD - 1, 1) + pltpu.roll(tile, HD - 2, 1))
        sums.append(pltpu.roll(tile, HD - 3, 1) + pltpu.roll(tile, HD - 4, 1))
    peak = stat
    for j in range(NEAR):
        peak = jnp.maximum(peak, tops[j])
    own = jnp.exp(stat - peak)
    row_sum = own * pltpu.roll(stat, HD - 1, 1)
    scales = []
    for j in range(NEAR):
        scale = jnp.exp(tops[j] - peak)
        row_sum = row_sum + scale * sums[j]
        scales.append(scale)
    for r in range(REQ):
        at = slice(r * 16, r * 16 + 16)

        def spread(tile):
            return jnp.broadcast_to(tile[:, r * 8 : r * 8 + 1], (16, HD))

        acc = spread(own) * acc_ref[at, :]
        for j in range(NEAR):
            acc = acc + spread(scales[j]) * recv_ref[j, at, :].astype(jnp.float32)
        total_ref[at, :] = acc / spread(row_sum)
    for h in range(QPK):
        tile = total_ref[pl.ds(h, 8, stride=QPK), :].astype(jnp.bfloat16)
        for r in range(REQ):
            out_ref[0, 0, r, :, h * HD : (h + 1) * HD] = tile[r * POS : (r + 1) * POS]


def local(hidden, gain, wqkv, pool, lengths, block_table, mig_blocks, mig_count):
    bf16, f32 = jnp.bfloat16, jnp.float32
    shape = jax.ShapeDtypeStruct
    params = pltpu.CompilerParams
    ids = jnp.transpose(mig_blocks, (0, 1, 3, 4, 2))
    counts = jnp.transpose(mig_count, (0, 1, 3, 2))
    blocks = pool[0, 0]
    swap = [(i, i ^ 1) for i in range(N)]
    other_ids = lax.ppermute(ids, "inst", swap)
    other_counts = lax.ppermute(counts, "inst", swap)
    groups = [[i for i in range(N) if i % 2 == core] for core in range(2)]

    partial_value = pl.pallas_call(
        project_kernel,
        in_specs=[ANY, ANY, ANY],
        out_specs=VMEM,
        out_shape=shape((N, MSG, HD), f32),
        scratch_shapes=[
            pltpu.VMEM((ROWS, N * SHARE), bf16),
            pltpu.VMEM((SHARE,), bf16),
            pltpu.VMEM((SHARE, STEPS * WIDE), bf16),
            pltpu.VMEM((ROWS, SHARE), bf16),
            pltpu.SemaphoreType.DMA((PARTS * REQ + 1,)),
            pltpu.SemaphoreType.DMA((STEPS,)),
        ],
        compiler_params=params(vmem_limit_bytes=24 * MIB),
        cost_estimate=pl.CostEstimate(flops=2 * ROWS * SHARE * STEPS * WIDE, bytes_accessed=8 * MIB, transcendentals=ROWS),
        name="project",
    )(*(pltpu.with_memory_space_constraint(x, pltpu.MemorySpace.HBM) for x in (hidden, gain, wqkv)))
    partial_value = partial_value.astype(jnp.float16)
    partial_value, other_ids, other_counts, lent_blocks = lax.optimization_barrier(
        (partial_value, other_ids, other_counts, blocks)
    )
    other_blocks = lax.ppermute(lent_blocks, "inst", swap)
    summands = lax.all_to_all(partial_value, "tp", split_axis=0, concat_axis=0, tiled=True)
    total = jnp.sum(summands.astype(f32), axis=0)
    total, other_blocks = lax.optimization_barrier((total, other_blocks))
    ask, new = pl.pallas_call(
        ask_kernel,
        in_specs=[VMEM, VMEM, VMEM, VMEM],
        out_specs=[VMEM, VMEM],
        out_shape=[shape((NEAR, ASK, HD), f32), shape((16, HD), f32)],
        compiler_params=params(vmem_limit_bytes=16 * MIB),
        name="ask",
    )(lengths, counts, other_counts, total)
    asked = lax.all_to_all(ask, "inst", split_axis=0, concat_axis=0, tiled=True, axis_index_groups=groups)
    answers, queries, new = pl.pallas_call(
        lent_kernel,
        in_specs=[ANY, ANY, ANY, ANY, VMEM, VMEM, VMEM, VMEM],
        out_specs=[VMEM, VMEM, VMEM],
        out_shape=[shape((NEAR, MSG, HD), bf16), shape((QROWS, HD), bf16), shape((16, HD), bf16)],
        scratch_shapes=[
            pltpu.VMEM((NEAR, QROWS, HD), bf16),
            pltpu.VMEM((NEAR * REQ, 2, 16, 2 * BLK), f32),
            pltpu.VMEM((NEAR * REQ, 2, 16, 2 * BLK), bf16),
            pltpu.SMEM((2, REQ, MCAP, N), jnp.int32),
            pltpu.SMEM((2, REQ, N), jnp.int32),
            pltpu.SemaphoreType.DMA((2, 2)),
        ],
        compiler_params=params(vmem_limit_bytes=24 * MIB),
        name="lent",
    )(ids, counts, other_ids, other_counts, asked, new, blocks, other_blocks)
    acc, stat = pl.pallas_call(
        resident_kernel,
        in_specs=[ANY, ANY, VMEM, VMEM, ANY],
        out_specs=[VMEM, VMEM],
        out_shape=[shape((QROWS, HD), f32), shape((16, HD), f32)],
        scratch_shapes=[
            pltpu.VMEM((REQ, 16, (MAXB + 1) * BLK), f32),
            pltpu.VMEM((REQ * MAXB, BLK, 2 * HD), bf16),
            pltpu.SMEM((PARTS, REQ), jnp.int32),
            pltpu.SMEM((REQ, MAXB), jnp.int32),
            pltpu.SemaphoreType.DMA((REQ,)),
            pltpu.SemaphoreType.DMA((2,)),
        ],
        compiler_params=params(vmem_limit_bytes=24 * MIB),
        cost_estimate=pl.CostEstimate(flops=100 * MIB * 8, bytes_accessed=16 * MIB, transcendentals=MIB),
        name="resident",
    )(lengths, block_table, queries, new, pltpu.with_memory_space_constraint(blocks, pltpu.MemorySpace.HBM))
    arrived = lax.all_to_all(answers, "inst", split_axis=0, concat_axis=0, tiled=True, axis_index_groups=groups)
    return pl.pallas_call(
        combine_kernel,
        in_specs=[VMEM, VMEM, VMEM],
        out_specs=VMEM,
        out_shape=shape((1, 1, REQ, POS, WIDE), bf16),
        scratch_shapes=[pltpu.VMEM((QROWS, HD), f32)],
        compiler_params=params(vmem_limit_bytes=16 * MIB),
        name="combine",
    )(arrived, acc, stat)


def solution(mesh):
    placed = (
        P("inst", None, None),
        P("tp"),
        P("tp", None),
        P("inst", "tp", None, None, None),
        P("inst", None, None),
        P("inst", None, None, None),
        P("inst", None, None, None, None),
        P("inst", None, None, None),
    )
    return jax.shard_map(
        local,
        mesh=mesh,
        in_specs=placed,
        out_specs=P("inst", "tp", None, None, None),
        check_vma=False,
    )
```

```python
import math

import numpy as np
import jax
import jax.numpy as jnp
from jax import lax
from jax.experimental import pallas as pl
from jax.experimental.pallas import tpu as pltpu
from jax.sharding import PartitionSpec as P

HEADS = 32
KVH = 4
HD = 128
QPK = 8
PARTS = 4
REQ = 4
POS = 2
MAXB = 24
MCAP = 2
BLK = 128
POOL = 128
N = 16
NEAR = N // 2
ROWS = PARTS * REQ * POS
QROWS = REQ * POS * QPK
SHARE = 512
WIDE = QPK * HD
MSG = 80
ASK = 72
ROOT = 1.0 / math.sqrt(HD)
EPSILON = 1e-05
NEGATIVE = -1e30
ROPE_BASE = 500000.0
MIB = 1 << 20
STEPS = 5
FLIGHT = 3
TURN = 4

FREQUENCY = np.exp(np.arange(HD // 2) * (-2.0 * math.log(ROPE_BASE) / HD)).astype(np.float32)

VMEM = pl.BlockSpec(memory_space=pltpu.VMEM)
ANY = pl.BlockSpec(memory_space=pl.ANY)


def own_part():
    return lax.axis_index("tp") % PARTS


def project_kernel(hidden, gain, w, *refs):
    out_refs, (hidden_ref, gain_ref, w_ref, normed_ref, y_ref, hidden_sem, w_sem) = refs[:PARTS], refs[PARTS:]
    hidden_copies = [
        pltpu.make_async_copy(hidden.at[a], hidden_ref.at[pl.ds(POS * a, POS), :], hidden_sem.at[a])
        for a in range(PARTS * REQ)
    ]
    hidden_copies.append(pltpu.make_async_copy(gain, gain_ref, hidden_sem.at[PARTS * REQ]))
    for copy in hidden_copies:
        copy.start()
    w_copies = [
        pltpu.make_async_copy(w.at[:, pl.ds(c * WIDE, WIDE)], w_ref.at[:, pl.ds(c * WIDE, WIDE)], w_sem.at[c])
        for c in range(STEPS)
    ]
    for copy in w_copies[:FLIGHT]:
        copy.start()
    for copy in hidden_copies:
        copy.wait()
    rows = hidden_ref[...].astype(jnp.float32)
    inv = lax.rsqrt(jnp.sum(rows * rows, axis=-1, keepdims=True) / rows.shape[1] + EPSILON)
    at = pl.multiple_of(lax.axis_index("tp") * SHARE, SHARE)
    own = hidden_ref[:, pl.ds(at, SHARE)].astype(jnp.float32)
    normed_ref[...] = (own * inv * gain_ref[...].astype(jnp.float32)[None, :]).astype(jnp.bfloat16)
    high, part = lax.axis_index("tp") // PARTS, own_part()
    for c in range(STEPS):
        w_copies[c].wait()
        if c + FLIGHT < STEPS:
            w_copies[c + FLIGHT].start()
        y_ref[c % 2] = jnp.dot(
            normed_ref[...], w_ref[:, c * WIDE : (c + 1) * WIDE], preferred_element_type=jnp.float32
        )
        for away, out_ref in enumerate(out_refs):
            at = pl.multiple_of(lax.rem(part + away, PARTS) * 8, 8)
            for u in range(QPK):
                if c < KVH:
                    group, chunk = c, u
                else:
                    group, chunk = u % KVH, QPK + u // KVH
                slot = lax.rem(group - high + KVH, KVH)
                out_ref[slot, chunk * 8 : chunk * 8 + 8, :] = y_ref[c % 2, pl.ds(at, 8), u * HD : u * HD + HD]


def ask_kernel(lengths, counts, other_count_ref, total_ref, ask_ref, new_ref, lengths_ref, count_ref, sem):
    part = own_part()
    me = lax.axis_index("inst")
    copies = [
        pltpu.make_async_copy(lengths.at[0], lengths_ref, sem.at[0]),
        pltpu.make_async_copy(counts.at[0, part], count_ref, sem.at[1]),
    ]
    for copy in copies:
        copy.start()
    for copy in copies:
        copy.wait()
    total = total_ref[...]
    counts = count_ref[...] + other_count_ref[0, part]
    lengths = lengths_ref[pl.ds(part, 1), :]
    row = lax.broadcasted_iota(jnp.int32, (8, N), 0)
    lane = lax.broadcasted_iota(jnp.int32, (8, N), 1)
    terms = jnp.zeros((8, N), jnp.int32)
    for r in range(REQ):
        lent = jnp.broadcast_to(counts[r : r + 1], (8, N)) * BLK
        own = jnp.where(lane == me, jnp.broadcast_to(lengths[:, r : r + 1], (8, N)) + row % POS, 0)
        terms = jnp.where(row // POS == r, lent + own, terms)
    terms = jnp.concatenate([terms.astype(jnp.float32), jnp.zeros((8, HD - N), jnp.float32)], axis=1)
    new_ref[...] = total[64:80]
    tiles = []
    for h in range(QPK):
        ask_ref[0, h * 8 : h * 8 + 8, :] = total[h * 8 : h * 8 + 8]
    for at in range(REQ * POS):
        tiles.append(ask_ref[0, pl.ds(at, QPK, stride=8), :])
    tiles.append(terms)
    whole = jnp.concatenate(tiles, axis=0)
    for i in range(NEAR):
        ask_ref[i] = whole


def rotated(x, cosine, sine):
    return x * cosine + pltpu.roll(x, HD // 2, 1) * sine


def dot_t(a, b):
    return lax.dot_general(a, b, (((1,), (1,)), ((), ())), preferred_element_type=jnp.float32)


def stats_tile(tile, r, columns):
    lane = lax.broadcasted_iota(jnp.int32, (16, HD), 1)
    for k, column in enumerate(columns):
        tile = jnp.where(lane == r * 8 + k, column, tile)
    return tile


def resident_kernel(
    lengths, table, q_ref, new_ref, pool, acc_ref, stat_ref, score_ref, blocks_ref, lengths_ref, table_ref, sem, int_sem
):
    part = own_part()
    copies = [
        pltpu.make_async_copy(table.at[0, part], table_ref, int_sem.at[0]),
        pltpu.make_async_copy(lengths.at[0], lengths_ref, int_sem.at[1]),
    ]
    for copy in copies:
        copy.start()
    for copy in copies:
        copy.wait()
    for r in range(REQ):
        for b in range(MAXB):
            pltpu.make_async_copy(pool.at[table_ref[r, b]], blocks_ref.at[r * MAXB + b], sem.at[r]).start()
    new = new_ref[...].astype(jnp.float32)
    pad = jnp.zeros((HD - 8, HD), jnp.float32)
    key_new = jnp.concatenate([new[:8], pad], axis=0).astype(jnp.bfloat16)
    value_new = jnp.concatenate([new[8:], pad], axis=0).astype(jnp.bfloat16)
    lane = lax.broadcasted_iota(jnp.int32, (16, 2 * BLK), 1)
    lane_new = lax.broadcasted_iota(jnp.int32, (16, BLK), 1)
    position = lax.broadcasted_iota(jnp.int32, (16, BLK), 0) // QPK
    tile = jnp.zeros((16, HD), jnp.float32)
    for r in range(REQ):
        query = q_ref[r * 16 : r * 16 + 16, :]
        length = lengths_ref[part, r]
        scores = jnp.where(
            (lane_new >= r * POS) & (lane_new <= r * POS + position), dot_t(query, key_new) * ROOT, NEGATIVE
        )
        score_ref[r, :, MAXB * BLK :] = scores
        top = jnp.max(scores, axis=-1, keepdims=True)
        most = jnp.full((16, 2 * BLK), NEGATIVE, jnp.float32)

        here = pl.ds(r * MAXB, MAXB)
        pltpu.make_async_copy(pool.at[pl.ds(0, MAXB)], blocks_ref.at[here], sem.at[r]).wait()

        def pair(b, first):
            at = r * MAXB + b
            return blocks_ref[at : at + 2, :, first : first + HD].reshape(2 * BLK, HD)

        for b in range(0, MAXB, 2):
            scores = jnp.where(lane + b * BLK < length, dot_t(query, pair(b, 0)) * ROOT, NEGATIVE)
            score_ref[r, :, b * BLK : (b + 2) * BLK] = scores
            most = jnp.maximum(most, scores)
        top = jnp.maximum(top, jnp.max(most, axis=-1, keepdims=True))
        weights = jnp.exp(score_ref[r, :, MAXB * BLK :] - top)
        row_sum = jnp.sum(weights, axis=-1, keepdims=True)
        acc = jnp.dot(weights.astype(jnp.bfloat16), value_new, preferred_element_type=jnp.float32)
        sums = jnp.zeros((16, 2 * BLK), jnp.float32)
        for b in range(0, MAXB, 2):
            weights = jnp.exp(score_ref[r, :, b * BLK : (b + 2) * BLK] - top)
            sums = sums + weights
            acc = acc + jnp.dot(weights.astype(jnp.bfloat16), pair(b, HD), preferred_element_type=jnp.float32)
        row_sum = row_sum + jnp.sum(sums, axis=-1, keepdims=True)
        acc_ref[r * 16 : r * 16 + 16, :] = acc
        tile = stats_tile(tile, r, (top, row_sum))
    stat_ref[...] = tile


def rounded(x):
    return x.astype(jnp.bfloat16).astype(jnp.float32)


def lent_kernel(
    ids,
    counts,
    other_ids,
    other_counts,
    ask_ref,
    new_ref,
    pool,
    other_pool_ref,
    out_ref,
    own_ref,
    own_new_ref,
    q_ref,
    score_ref,
    weight_ref,
    ids_ref,
    count_ref,
    blocks_ref,
    sem,
    block_sem,
):
    part = own_part()
    copies = [
        pltpu.make_async_copy(whole.at[0, part], table.at[side], sem.at[at, side])
        for at, (table, both) in enumerate(((ids_ref, (ids, other_ids)), (count_ref, (counts, other_counts))))
        for side, whole in enumerate(both)
    ]
    for copy in copies:
        copy.start()
    me = lax.axis_index("inst")
    core = lax.rem(me, 2)
    copies[0].wait()
    for n in range(NEAR * REQ):
        for b in range(MCAP):
            block = pool.at[ids_ref[0, n % REQ, b, 2 * (n // REQ) + core]]
            pltpu.make_async_copy(block, blocks_ref.at[n * MCAP + b], block_sem.at[n // (TURN * REQ)]).start()

    lane = lax.broadcasted_iota(jnp.int32, (8, HD), 1)
    low = lane < HD // 2
    frequency = jnp.zeros((8, HD), jnp.float32)
    for m in range(HD // 2):
        frequency = jnp.where(lane % (HD // 2) == m, float(FREQUENCY[m]), frequency)
    positions = ask_ref[0, QROWS:ASK, :]
    for k in range(1, NEAR):
        positions = positions + ask_ref[k, QROWS:ASK, :]

    def position(k):
        return jnp.where(core == 0, positions[:, 2 * k : 2 * k + 1], positions[:, 2 * k + 1 : 2 * k + 2])

    for first in range(NEAR // 2):
        second = first + NEAR // 2
        angle = jnp.where(low, position(first), position(second)) * frequency
        cosine, sine = jnp.cos(angle), jnp.sin(angle)
        cosine_turned, sine_turned = pltpu.roll(cosine, HD // 2, 1), pltpu.roll(sine, HD // 2, 1)
        for k, cos, sin in (
            (first, jnp.where(low, cosine, cosine_turned), jnp.where(low, -sine, sine_turned)),
            (second, jnp.where(low, cosine_turned, cosine), jnp.where(low, -sine_turned, sine)),
        ):
            for r in range(REQ):
                both = []
                for at in range(r * POS, r * POS + POS):
                    x = ask_ref[k, at * QPK : at * QPK + QPK, :]
                    both.append(rotated(x, cos[at : at + 1], sin[at : at + 1]))
                q_ref[k, r * 16 : r * 16 + 16, :] = jnp.concatenate(both, axis=0).astype(jnp.bfloat16)
    own_ref[...] = q_ref[me // 2]
    own = jnp.sum(jnp.where(lane == me, positions, 0.0), axis=-1, keepdims=True)
    angle = own * frequency
    sine = jnp.sin(angle)
    key = rotated(new_ref[:8], jnp.cos(angle), jnp.where(low, -sine, sine))
    own_new_ref[...] = jnp.concatenate([key, new_ref[8:]], axis=0).astype(jnp.bfloat16)

    for copy in copies[1:]:
        copy.wait()
    lane = lax.broadcasted_iota(jnp.int32, (16, 2 * BLK), 1)

    def valid(n, side):
        return lane < count_ref[side, n % REQ, 2 * (n // REQ) + core] * BLK

    def pair(n, side, first):
        if side == 0:
            return blocks_ref[n * MCAP : (n + 1) * MCAP, :, first : first + HD].reshape(MCAP * BLK, HD)
        at = 2 * (n // REQ) + core
        halves = [other_pool_ref[ids_ref[1, n % REQ, b, at], :, first : first + HD] for b in range(MCAP)]
        return jnp.concatenate(halves, axis=0)

    def score(n, side):
        query = q_ref[n // REQ, n % REQ * 16 : n % REQ * 16 + 16, :]
        score_ref[n, side] = jnp.where(valid(n, side), dot_t(query, pair(n, side, 0)) * ROOT, NEGATIVE)

    for n in range(NEAR * REQ):
        score(n, 1)
    for start in range(0, NEAR * REQ, TURN * REQ):
        group = range(start, start + TURN * REQ)
        here = pl.ds(start * MCAP, TURN * REQ * MCAP)
        pltpu.make_async_copy(pool.at[pl.ds(0, TURN * REQ * MCAP)], blocks_ref.at[here], block_sem.at[start // (TURN * REQ)]).wait()
        for n in group:
            score(n, 0)
        for n in group:
            r = n % REQ
            if r == 0:
                tile = jnp.zeros((16, HD), jnp.float32)
            top = jnp.max(jnp.maximum(score_ref[n, 0], score_ref[n, 1]), axis=-1, keepdims=True)
            row_sum = jnp.zeros((16, 2 * BLK), jnp.float32)
            for side in range(2):
                weights = jnp.where(valid(n, side), jnp.exp(score_ref[n, side] - top), 0.0)
                row_sum = row_sum + weights
                weight_ref[n, side] = weights.astype(jnp.bfloat16)
            row_sum = jnp.sum(row_sum, axis=-1, keepdims=True)
            high = rounded(top)
            middle = rounded(top - high)
            sum_high = rounded(row_sum)
            tile = stats_tile(tile, r, (high, middle, top - high - middle, sum_high, row_sum - sum_high))
            if r == REQ - 1:
                out_ref[n // REQ, 64:80, :] = tile.astype(jnp.bfloat16)
        for n in group:
            acc = jnp.dot(weight_ref[n, 0], pair(n, 0, HD), preferred_element_type=jnp.float32)
            acc = acc + jnp.dot(weight_ref[n, 1], pair(n, 1, HD), preferred_element_type=jnp.float32)
            out_ref[n // REQ, n % REQ * 16 : n % REQ * 16 + 16, :] = acc.astype(jnp.bfloat16)


def combine_kernel(recv_ref, acc_ref, stat_ref, out_ref, total_ref):
    stat = stat_ref[...]
    tops, sums = [], []
    for j in range(NEAR):
        tile = recv_ref[j, 64:80, :].astype(jnp.float32)
        tops.append(tile + pltpu.roll(tile, HD - 1, 1) + pltpu.roll(tile, HD - 2, 1))
        sums.append(pltpu.roll(tile, HD - 3, 1) + pltpu.roll(tile, HD - 4, 1))
    peak = stat
    for j in range(NEAR):
        peak = jnp.maximum(peak, tops[j])
    own = jnp.exp(stat - peak)
    row_sum = own * pltpu.roll(stat, HD - 1, 1)
    scales = []
    for j in range(NEAR):
        scale = jnp.exp(tops[j] - peak)
        row_sum = row_sum + scale * sums[j]
        scales.append(scale)
    for r in range(REQ):
        at = slice(r * 16, r * 16 + 16)

        def spread(tile):
            return jnp.broadcast_to(tile[:, r * 8 : r * 8 + 1], (16, HD))

        acc = spread(own) * acc_ref[at, :]
        for j in range(NEAR):
            acc = acc + spread(scales[j]) * recv_ref[j, at, :].astype(jnp.float32)
        total_ref[at, :] = acc / spread(row_sum)
    for h in range(QPK):
        tile = total_ref[pl.ds(h, 8, stride=QPK), :].astype(jnp.bfloat16)
        for r in range(REQ):
            out_ref[0, 0, r, :, h * HD : (h + 1) * HD] = tile[r * POS : (r + 1) * POS]


def local(hidden, gain, wqkv, pool, lengths, block_table, mig_blocks, mig_count):
    bf16, f32 = jnp.bfloat16, jnp.float32
    shape = jax.ShapeDtypeStruct
    params = pltpu.CompilerParams
    ids = jnp.transpose(mig_blocks, (0, 1, 3, 4, 2))
    counts = jnp.transpose(mig_count, (0, 1, 3, 2))
    blocks = pool[0, 0]

    def fixed(*arrays):
        return (pltpu.with_memory_space_constraint(x, pltpu.MemorySpace.HBM) for x in arrays)

    swap = [(i, i ^ 1) for i in range(N)]
    other_ids = lax.ppermute(ids, "inst", swap)
    other_counts = lax.ppermute(counts, "inst", swap)
    groups = [[i for i in range(N) if i % 2 == core] for core in range(2)]

    partial_values = pl.pallas_call(
        project_kernel,
        in_specs=[ANY, ANY, ANY],
        out_specs=[VMEM] * PARTS,
        out_shape=[shape((KVH, MSG, HD), f32)] * PARTS,
        scratch_shapes=[
            pltpu.VMEM((ROWS, N * SHARE), bf16),
            pltpu.VMEM((SHARE,), bf16),
            pltpu.VMEM((SHARE, STEPS * WIDE), bf16),
            pltpu.VMEM((ROWS, SHARE), bf16),
            pltpu.VMEM((2, ROWS, WIDE), f32),
            pltpu.SemaphoreType.DMA((PARTS * REQ + 1,)),
            pltpu.SemaphoreType.DMA((STEPS,)),
        ],
        compiler_params=params(vmem_limit_bytes=24 * MIB),
        cost_estimate=pl.CostEstimate(flops=2 * ROWS * SHARE * STEPS * WIDE, bytes_accessed=8 * MIB, transcendentals=ROWS),
        name="project",
    )(*fixed(hidden, gain, wqkv))
    partial_values, other_ids, other_counts, lent_blocks = lax.optimization_barrier(
        (partial_values, other_ids, other_counts, blocks)
    )
    other_blocks = lax.ppermute(lent_blocks, "inst", swap)

    def towards(x, by_part, by_group):
        pairs = [
            (g * PARTS + p, (g + by_group) % KVH * PARTS + (p + by_part) % PARTS) for g in range(KVH) for p in range(PARTS)
        ]
        return lax.ppermute(x, "tp", pairs)

    came = [towards(partial_values[away], away, 0) for away in (1, 3, 2)]
    sums = [partial_values[0][m] + came[0][m] + came[1][m] + came[2][m] for m in range(KVH)]
    came = [towards(sums[away], 0, away) for away in (2, 1, 3)]
    total = sums[0] + came[0] + came[1] + came[2]
    total, other_blocks = lax.optimization_barrier((total, other_blocks))
    ask, new = pl.pallas_call(
        ask_kernel,
        in_specs=[ANY, ANY, VMEM, VMEM],
        out_specs=[VMEM, VMEM],
        out_shape=[shape((NEAR, ASK, HD), f32), shape((16, HD), f32)],
        scratch_shapes=[
            pltpu.VMEM((PARTS, REQ), jnp.int32),
            pltpu.VMEM((REQ, N), jnp.int32),
            pltpu.SemaphoreType.DMA((2,)),
        ],
        compiler_params=params(vmem_limit_bytes=16 * MIB),
        name="ask",
    )(*fixed(lengths, counts), other_counts, total)
    asked = lax.all_to_all(ask, "inst", split_axis=0, concat_axis=0, tiled=True, axis_index_groups=groups)
    answers, queries, new = pl.pallas_call(
        lent_kernel,
        in_specs=[ANY, ANY, ANY, ANY, VMEM, VMEM, ANY, VMEM],
        out_specs=[VMEM, VMEM, VMEM],
        out_shape=[shape((NEAR, MSG, HD), bf16), shape((QROWS, HD), bf16), shape((16, HD), bf16)],
        scratch_shapes=[
            pltpu.VMEM((NEAR, QROWS, HD), bf16),
            pltpu.VMEM((NEAR * REQ, 2, 16, 2 * BLK), f32),
            pltpu.VMEM((NEAR * REQ, 2, 16, 2 * BLK), bf16),
            pltpu.SMEM((2, REQ, MCAP, N), jnp.int32),
            pltpu.SMEM((2, REQ, N), jnp.int32),
            pltpu.VMEM((NEAR * REQ * MCAP, BLK, 2 * HD), bf16),
            pltpu.SemaphoreType.DMA((2, 2)),
            pltpu.SemaphoreType.DMA((NEAR // TURN,)),
        ],
        compiler_params=params(vmem_limit_bytes=24 * MIB),
        name="lent",
    )(*fixed(ids, counts), other_ids, other_counts, asked, new, *fixed(blocks), other_blocks)
    acc, stat = pl.pallas_call(
        resident_kernel,
        in_specs=[ANY, ANY, VMEM, VMEM, ANY],
        out_specs=[VMEM, VMEM],
        out_shape=[shape((QROWS, HD), f32), shape((16, HD), f32)],
        scratch_shapes=[
            pltpu.VMEM((REQ, 16, (MAXB + 1) * BLK), f32),
            pltpu.VMEM((REQ * MAXB, BLK, 2 * HD), bf16),
            pltpu.SMEM((PARTS, REQ), jnp.int32),
            pltpu.SMEM((REQ, MAXB), jnp.int32),
            pltpu.SemaphoreType.DMA((REQ,)),
            pltpu.SemaphoreType.DMA((2,)),
        ],
        compiler_params=params(vmem_limit_bytes=24 * MIB),
        cost_estimate=pl.CostEstimate(flops=100 * MIB * 8, bytes_accessed=16 * MIB, transcendentals=MIB),
        name="resident",
    )(*fixed(lengths, block_table), queries, new, *fixed(blocks))
    arrived = lax.all_to_all(answers, "inst", split_axis=0, concat_axis=0, tiled=True, axis_index_groups=groups)
    return pl.pallas_call(
        combine_kernel,
        in_specs=[VMEM, VMEM, VMEM],
        out_specs=VMEM,
        out_shape=shape((1, 1, REQ, POS, WIDE), bf16),
        scratch_shapes=[pltpu.VMEM((QROWS, HD), f32)],
        compiler_params=params(vmem_limit_bytes=16 * MIB),
        name="combine",
    )(arrived, acc, stat)


def solution(mesh):
    placed = (
        P("inst", None, None),
        P("tp"),
        P("tp", None),
        P("inst", "tp", None, None, None),
        P("inst", None, None),
        P("inst", None, None, None),
        P("inst", None, None, None, None),
        P("inst", None, None, None),
    )
    return jax.shard_map(
        local,
        mesh=mesh,
        in_specs=placed,
        out_specs=P("inst", "tp", None, None, None),
        check_vma=False,
    )
```

```python
import math

import numpy as np
import jax
import jax.numpy as jnp
from jax import lax
from jax.experimental import pallas as pl
from jax.experimental.pallas import tpu as pltpu
from jax.sharding import PartitionSpec as P

HEADS = 32
KVH = 4
HD = 128
QPK = 8
PARTS = 4
REQ = 4
POS = 2
MAXB = 24
MCAP = 2
BLK = 128
POOL = 128
N = 16
NEAR = N // 2
ROWS = PARTS * REQ * POS
QROWS = REQ * POS * QPK
SHARE = 512
WIDE = QPK * HD
MSG = 80
ASK = 72
ROOT = 1.0 / math.sqrt(HD)
EPSILON = 1e-05
NEGATIVE = -1e30
ROPE_BASE = 500000.0
MIB = 1 << 20
STEPS = 5
FLIGHT = 3
TURN = 4
LEVEL = 128.0

FREQUENCY = np.exp(np.arange(HD // 2) * (-2.0 * math.log(ROPE_BASE) / HD)).astype(np.float32)

VMEM = pl.BlockSpec(memory_space=pltpu.VMEM)
ANY = pl.BlockSpec(memory_space=pl.ANY)


def own_part():
    return lax.axis_index("tp") % PARTS


def project_kernel(hidden, gain, w, out_ref, hidden_ref, gain_ref, w_ref, normed_ref, hidden_sem, w_sem):
    hidden_copies = [
        pltpu.make_async_copy(hidden, hidden_ref, hidden_sem.at[0]),
        pltpu.make_async_copy(gain, gain_ref, hidden_sem.at[1]),
    ]
    for copy in hidden_copies:
        copy.start()
    w_copies = [
        pltpu.make_async_copy(w.at[:, pl.ds(c * WIDE, WIDE)], w_ref.at[:, pl.ds(c * WIDE, WIDE)], w_sem.at[c])
        for c in range(STEPS)
    ]
    for copy in w_copies[:FLIGHT]:
        copy.start()
    for copy in hidden_copies:
        copy.wait()
    rows = hidden_ref[...].astype(jnp.float32)
    inv = lax.rsqrt(jnp.sum(rows * rows, axis=-1, keepdims=True) / rows.shape[2] + EPSILON)
    at = pl.multiple_of(lax.axis_index("tp") * SHARE, SHARE)
    own = (hidden_ref[:, :, pl.ds(at, SHARE)].astype(jnp.float32) * inv).reshape(ROWS, SHARE)
    normed_ref[...] = (own * gain_ref[...].astype(jnp.float32)[None, :]).astype(jnp.bfloat16)
    for c in range(STEPS):
        w_copies[c].wait()
        if c + FLIGHT < STEPS:
            w_copies[c + FLIGHT].start()
        y = LEVEL * jnp.dot(normed_ref[...], w_ref[:, c * WIDE : (c + 1) * WIDE], preferred_element_type=jnp.float32)
        for u in range(QPK):
            if c < KVH:
                group, chunk = c, u
            else:
                group, chunk = u % KVH, QPK + u // KVH
            for part in range(PARTS):
                out_ref[group * PARTS + part, chunk * 8 : chunk * 8 + 8, :] = y[
                    part * 8 : part * 8 + 8, u * HD : u * HD + HD
                ]


def ask_kernel(lengths_ref, count_ref, other_count_ref, total_ref, ask_ref, new_ref):
    part = own_part()
    me = lax.axis_index("inst")
    total = total_ref[...] * (1.0 / LEVEL)
    counts = count_ref[0, part] + other_count_ref[0, part]
    lengths = lengths_ref[0, pl.ds(part, 1), :]
    row = lax.broadcasted_iota(jnp.int32, (8, N), 0)
    lane = lax.broadcasted_iota(jnp.int32, (8, N), 1)
    terms = jnp.zeros((8, N), jnp.int32)
    for r in range(REQ):
        lent = jnp.broadcast_to(counts[r : r + 1], (8, N)) * BLK
        own = jnp.where(lane == me, jnp.broadcast_to(lengths[:, r : r + 1], (8, N)) + row % POS, 0)
        terms = jnp.where(row // POS == r, lent + own, terms)
    terms = jnp.concatenate([terms.astype(jnp.float32), jnp.zeros((8, HD - N), jnp.float32)], axis=1)
    new_ref[...] = total[64:80]
    tiles = []
    for h in range(QPK):
        ask_ref[0, h * 8 : h * 8 + 8, :] = total[h * 8 : h * 8 + 8]
    for at in range(REQ * POS):
        tiles.append(ask_ref[0, pl.ds(at, QPK, stride=8), :])
    tiles.append(terms)
    whole = jnp.concatenate(tiles, axis=0)
    for i in range(NEAR):
        ask_ref[i] = whole


def rotated(x, cosine, sine):
    return x * cosine + pltpu.roll(x, HD // 2, 1) * sine


def dot_t(a, b):
    return lax.dot_general(a, b, (((1,), (1,)), ((), ())), preferred_element_type=jnp.float32)


def stats_tile(tile, r, columns):
    lane = lax.broadcasted_iota(jnp.int32, (16, HD), 1)
    for k, column in enumerate(columns):
        tile = jnp.where(lane == r * 8 + k, column, tile)
    return tile


def resident_kernel(
    lengths, table, q_ref, new_ref, pool, acc_ref, stat_ref, score_ref, blocks_ref, lengths_ref, table_ref, sem, int_sem
):
    part = own_part()
    copies = [
        pltpu.make_async_copy(table.at[0, part], table_ref, int_sem.at[0]),
        pltpu.make_async_copy(lengths.at[0], lengths_ref, int_sem.at[1]),
    ]
    for copy in copies:
        copy.start()
    for copy in copies:
        copy.wait()
    for r in range(REQ):
        for b in range(MAXB):
            pltpu.make_async_copy(pool.at[table_ref[r, b]], blocks_ref.at[r * MAXB + b], sem.at[r]).start()
    new = new_ref[...].astype(jnp.float32)
    pad = jnp.zeros((HD - 8, HD), jnp.float32)
    key_new = jnp.concatenate([new[:8], pad], axis=0).astype(jnp.bfloat16)
    value_new = jnp.concatenate([new[8:], pad], axis=0).astype(jnp.bfloat16)
    lane = lax.broadcasted_iota(jnp.int32, (16, 2 * BLK), 1)
    lane_new = lax.broadcasted_iota(jnp.int32, (16, BLK), 1)
    position = lax.broadcasted_iota(jnp.int32, (16, BLK), 0) // QPK
    tile = jnp.zeros((16, HD), jnp.float32)
    for r in range(REQ):
        query = q_ref[r * 16 : r * 16 + 16, :]
        length = lengths_ref[part, r]
        scores = jnp.where(
            (lane_new >= r * POS) & (lane_new <= r * POS + position), dot_t(query, key_new) * ROOT, NEGATIVE
        )
        score_ref[r, :, MAXB * BLK :] = scores
        top = jnp.max(scores, axis=-1, keepdims=True)
        most = jnp.full((16, 2 * BLK), NEGATIVE, jnp.float32)

        here = pl.ds(r * MAXB, MAXB)
        pltpu.make_async_copy(pool.at[pl.ds(0, MAXB)], blocks_ref.at[here], sem.at[r]).wait()

        def pair(b, first):
            at = r * MAXB + b
            return blocks_ref[at : at + 2, :, first : first + HD].reshape(2 * BLK, HD)

        for b in range(0, MAXB, 2):
            scores = jnp.where(lane + b * BLK < length, dot_t(query, pair(b, 0)) * ROOT, NEGATIVE)
            score_ref[r, :, b * BLK : (b + 2) * BLK] = scores
            most = jnp.maximum(most, scores)
        top = jnp.maximum(top, jnp.max(most, axis=-1, keepdims=True))
        weights = jnp.exp(score_ref[r, :, MAXB * BLK :] - top)
        row_sum = jnp.sum(weights, axis=-1, keepdims=True)
        acc = jnp.dot(weights.astype(jnp.bfloat16), value_new, preferred_element_type=jnp.float32)
        sums = jnp.zeros((16, 2 * BLK), jnp.float32)
        for b in range(0, MAXB, 2):
            weights = jnp.exp(score_ref[r, :, b * BLK : (b + 2) * BLK] - top)
            sums = sums + weights
            acc = acc + jnp.dot(weights.astype(jnp.bfloat16), pair(b, HD), preferred_element_type=jnp.float32)
        row_sum = row_sum + jnp.sum(sums, axis=-1, keepdims=True)
        acc_ref[r * 16 : r * 16 + 16, :] = acc
        tile = stats_tile(tile, r, (top, row_sum))
    stat_ref[...] = tile


def rounded(x):
    return x.astype(jnp.bfloat16).astype(jnp.float32)


def lent_kernel(
    ids,
    counts,
    other_ids,
    other_counts,
    ask_ref,
    new_ref,
    pool_ref,
    other_pool_ref,
    out_ref,
    own_ref,
    own_new_ref,
    q_ref,
    score_ref,
    weight_ref,
    ids_ref,
    count_ref,
    sem,
):
    part = own_part()
    copies = [
        pltpu.make_async_copy(whole.at[0, part], table.at[side], sem.at[at, side])
        for at, (table, both) in enumerate(((ids_ref, (ids, other_ids)), (count_ref, (counts, other_counts))))
        for side, whole in enumerate(both)
    ]
    for copy in copies:
        copy.start()
    me = lax.axis_index("inst")
    core = lax.rem(me, 2)
    pools = (pool_ref, other_pool_ref)

    lane = lax.broadcasted_iota(jnp.int32, (8, HD), 1)
    low = lane < HD // 2
    frequency = jnp.zeros((8, HD), jnp.float32)
    for m in range(HD // 2):
        frequency = jnp.where(lane % (HD // 2) == m, float(FREQUENCY[m]), frequency)
    positions = ask_ref[0, QROWS:ASK, :]
    for k in range(1, NEAR):
        positions = positions + ask_ref[k, QROWS:ASK, :]

    def position(k):
        return jnp.where(core == 0, positions[:, 2 * k : 2 * k + 1], positions[:, 2 * k + 1 : 2 * k + 2])

    for first in range(NEAR // 2):
        second = first + NEAR // 2
        angle = jnp.where(low, position(first), position(second)) * frequency
        cosine, sine = jnp.cos(angle), jnp.sin(angle)
        cosine_turned, sine_turned = pltpu.roll(cosine, HD // 2, 1), pltpu.roll(sine, HD // 2, 1)
        for k, cos, sin in (
            (first, jnp.where(low, cosine, cosine_turned), jnp.where(low, -sine, sine_turned)),
            (second, jnp.where(low, cosine_turned, cosine), jnp.where(low, -sine_turned, sine)),
        ):
            for r in range(REQ):
                both = []
                for at in range(r * POS, r * POS + POS):
                    x = ask_ref[k, at * QPK : at * QPK + QPK, :]
                    both.append(rotated(x, cos[at : at + 1], sin[at : at + 1]))
                q_ref[k, r * 16 : r * 16 + 16, :] = jnp.concatenate(both, axis=0).astype(jnp.bfloat16)
    own_ref[...] = q_ref[me // 2]
    own = jnp.sum(jnp.where(lane == me, positions, 0.0), axis=-1, keepdims=True)
    angle = own * frequency
    sine = jnp.sin(angle)
    key = rotated(new_ref[:8], jnp.cos(angle), jnp.where(low, -sine, sine))
    own_new_ref[...] = jnp.concatenate([key, new_ref[8:]], axis=0).astype(jnp.bfloat16)

    for copy in copies:
        copy.wait()
    lane = lax.broadcasted_iota(jnp.int32, (16, 2 * BLK), 1)

    def valid(n, side):
        return lane < count_ref[side, n % REQ, 2 * (n // REQ) + core] * BLK

    def pair(n, side, first):
        at = 2 * (n // REQ) + core
        halves = [pools[side][ids_ref[side, n % REQ, b, at], :, first : first + HD] for b in range(MCAP)]
        return jnp.concatenate(halves, axis=0)

    for start in range(0, NEAR * REQ, TURN * REQ):
        group = range(start, start + TURN * REQ)
        for n in group:
            query = q_ref[n // REQ, n % REQ * 16 : n % REQ * 16 + 16, :]
            for side in range(2):
                score_ref[n, side] = jnp.where(valid(n, side), dot_t(query, pair(n, side, 0)) * ROOT, NEGATIVE)
        for n in group:
            r = n % REQ
            if r == 0:
                tile = jnp.zeros((16, HD), jnp.float32)
            top = jnp.max(jnp.maximum(score_ref[n, 0], score_ref[n, 1]), axis=-1, keepdims=True)
            row_sum = jnp.zeros((16, 2 * BLK), jnp.float32)
            for side in range(2):
                weights = jnp.where(valid(n, side), jnp.exp(score_ref[n, side] - top), 0.0)
                row_sum = row_sum + weights
                weight_ref[n, side] = weights.astype(jnp.bfloat16)
            row_sum = jnp.sum(row_sum, axis=-1, keepdims=True)
            high = rounded(top)
            middle = rounded(top - high)
            sum_high = rounded(row_sum)
            tile = stats_tile(tile, r, (high, middle, top - high - middle, sum_high, row_sum - sum_high))
            if r == REQ - 1:
                out_ref[n // REQ, 64:80, :] = tile.astype(jnp.bfloat16)
        for n in group:
            acc = jnp.dot(weight_ref[n, 0], pair(n, 0, HD), preferred_element_type=jnp.float32)
            acc = acc + jnp.dot(weight_ref[n, 1], pair(n, 1, HD), preferred_element_type=jnp.float32)
            out_ref[n // REQ, n % REQ * 16 : n % REQ * 16 + 16, :] = acc.astype(jnp.bfloat16)


def combine_kernel(recv_ref, acc_ref, stat_ref, out_ref, total_ref):
    stat = stat_ref[...]
    tops, sums = [], []
    for j in range(NEAR):
        tile = recv_ref[j, 64:80, :].astype(jnp.float32)
        tops.append(tile + pltpu.roll(tile, HD - 1, 1) + pltpu.roll(tile, HD - 2, 1))
        sums.append(pltpu.roll(tile, HD - 3, 1) + pltpu.roll(tile, HD - 4, 1))
    peak = stat
    for j in range(NEAR):
        peak = jnp.maximum(peak, tops[j])
    own = jnp.exp(stat - peak)
    row_sum = own * pltpu.roll(stat, HD - 1, 1)
    scales = []
    for j in range(NEAR):
        scale = jnp.exp(tops[j] - peak)
        row_sum = row_sum + scale * sums[j]
        scales.append(scale)
    for r in range(REQ):
        at = slice(r * 16, r * 16 + 16)

        def spread(tile):
            return jnp.broadcast_to(tile[:, r * 8 : r * 8 + 1], (16, HD))

        acc = spread(own) * acc_ref[at, :]
        for j in range(NEAR):
            acc = acc + spread(scales[j]) * recv_ref[j, at, :].astype(jnp.float32)
        total_ref[at, :] = acc / spread(row_sum)
    for h in range(QPK):
        tile = total_ref[pl.ds(h, 8, stride=QPK), :].astype(jnp.bfloat16)
        for r in range(REQ):
            out_ref[0, 0, r, :, h * HD : (h + 1) * HD] = tile[r * POS : (r + 1) * POS]


def local(hidden, gain, wqkv, pool, lengths, block_table, mig_blocks, mig_count):
    bf16, f32 = jnp.bfloat16, jnp.float32
    shape = jax.ShapeDtypeStruct
    params = pltpu.CompilerParams
    ids = jnp.transpose(mig_blocks, (0, 1, 3, 4, 2))
    counts = jnp.transpose(mig_count, (0, 1, 3, 2))
    blocks = pool[0, 0]
    swap = [(i, i ^ 1) for i in range(N)]
    other_ids = lax.ppermute(ids, "inst", swap)
    other_counts = lax.ppermute(counts, "inst", swap)
    groups = [[i for i in range(N) if i % 2 == core] for core in range(2)]

    partial_value = pl.pallas_call(
        project_kernel,
        in_specs=[ANY, ANY, ANY],
        out_specs=VMEM,
        out_shape=shape((N, MSG, HD), f32),
        scratch_shapes=[
            pltpu.VMEM((PARTS * REQ, POS, N * SHARE), bf16),
            pltpu.VMEM((SHARE,), bf16),
            pltpu.VMEM((SHARE, STEPS * WIDE), bf16),
            pltpu.VMEM((ROWS, SHARE), bf16),
            pltpu.SemaphoreType.DMA((2,)),
            pltpu.SemaphoreType.DMA((STEPS,)),
        ],
        compiler_params=params(vmem_limit_bytes=24 * MIB),
        cost_estimate=pl.CostEstimate(flops=2 * ROWS * SHARE * STEPS * WIDE, bytes_accessed=8 * MIB, transcendentals=ROWS),
        name="project",
    )(*(pltpu.with_memory_space_constraint(x, pltpu.MemorySpace.HBM) for x in (hidden, gain, wqkv)))
    partial_value = partial_value.astype(jnp.float16)
    partial_value, other_ids, other_counts, lent_blocks = lax.optimization_barrier(
        (partial_value, other_ids, other_counts, blocks)
    )
    other_blocks = lax.ppermute(lent_blocks, "inst", swap)
    summands = lax.all_to_all(partial_value, "tp", split_axis=0, concat_axis=0, tiled=True)
    total = jnp.sum(summands.astype(f32), axis=0)
    total, other_blocks = lax.optimization_barrier((total, other_blocks))
    ask, new = pl.pallas_call(
        ask_kernel,
        in_specs=[VMEM, VMEM, VMEM, VMEM],
        out_specs=[VMEM, VMEM],
        out_shape=[shape((NEAR, ASK, HD), f32), shape((16, HD), f32)],
        compiler_params=params(vmem_limit_bytes=16 * MIB),
        name="ask",
    )(lengths, counts, other_counts, total)
    asked = lax.all_to_all(ask, "inst", split_axis=0, concat_axis=0, tiled=True, axis_index_groups=groups)
    answers, queries, new = pl.pallas_call(
        lent_kernel,
        in_specs=[ANY, ANY, ANY, ANY, VMEM, VMEM, VMEM, VMEM],
        out_specs=[VMEM, VMEM, VMEM],
        out_shape=[shape((NEAR, MSG, HD), bf16), shape((QROWS, HD), bf16), shape((16, HD), bf16)],
        scratch_shapes=[
            pltpu.VMEM((NEAR, QROWS, HD), bf16),
            pltpu.VMEM((NEAR * REQ, 2, 16, 2 * BLK), f32),
            pltpu.VMEM((NEAR * REQ, 2, 16, 2 * BLK), bf16),
            pltpu.SMEM((2, REQ, MCAP, N), jnp.int32),
            pltpu.SMEM((2, REQ, N), jnp.int32),
            pltpu.SemaphoreType.DMA((2, 2)),
        ],
        compiler_params=params(vmem_limit_bytes=24 * MIB),
        name="lent",
    )(ids, counts, other_ids, other_counts, asked, new, blocks, other_blocks)
    acc, stat = pl.pallas_call(
        resident_kernel,
        in_specs=[ANY, ANY, VMEM, VMEM, ANY],
        out_specs=[VMEM, VMEM],
        out_shape=[shape((QROWS, HD), f32), shape((16, HD), f32)],
        scratch_shapes=[
            pltpu.VMEM((REQ, 16, (MAXB + 1) * BLK), f32),
            pltpu.VMEM((REQ * MAXB, BLK, 2 * HD), bf16),
            pltpu.SMEM((PARTS, REQ), jnp.int32),
            pltpu.SMEM((REQ, MAXB), jnp.int32),
            pltpu.SemaphoreType.DMA((REQ,)),
            pltpu.SemaphoreType.DMA((2,)),
        ],
        compiler_params=params(vmem_limit_bytes=24 * MIB),
        cost_estimate=pl.CostEstimate(flops=100 * MIB * 8, bytes_accessed=16 * MIB, transcendentals=MIB),
        name="resident",
    )(lengths, block_table, queries, new, pltpu.with_memory_space_constraint(blocks, pltpu.MemorySpace.HBM))
    arrived = lax.all_to_all(answers, "inst", split_axis=0, concat_axis=0, tiled=True, axis_index_groups=groups)
    return pl.pallas_call(
        combine_kernel,
        in_specs=[VMEM, VMEM, VMEM],
        out_specs=VMEM,
        out_shape=shape((1, 1, REQ, POS, WIDE), bf16),
        scratch_shapes=[pltpu.VMEM((QROWS, HD), f32)],
        compiler_params=params(vmem_limit_bytes=16 * MIB),
        name="combine",
    )(arrived, acc, stat)


def solution(mesh):
    placed = (
        P("inst", None, None),
        P("tp"),
        P("tp", None),
        P("inst", "tp", None, None, None),
        P("inst", None, None),
        P("inst", None, None, None),
        P("inst", None, None, None, None),
        P("inst", None, None, None),
    )
    return jax.shard_map(
        local,
        mesh=mesh,
        in_specs=placed,
        out_specs=P("inst", "tp", None, None, None),
        check_vma=False,
    )
```

```python
import math

import numpy as np
import jax
import jax.numpy as jnp
from jax import lax
from jax.experimental import pallas as pl
from jax.experimental.pallas import tpu as pltpu
from jax.sharding import PartitionSpec as P

HEADS = 32
KVH = 4
HD = 128
QPK = 8
PARTS = 4
REQ = 4
POS = 2
MAXB = 24
MCAP = 2
BLK = 128
POOL = 128
N = 16
NEAR = N // 2
ROWS = PARTS * REQ * POS
QROWS = REQ * POS * QPK
SHARE = 512
WIDE = QPK * HD
MSG = 80
ASK = 72
ROOT = 1.0 / math.sqrt(HD)
EPSILON = 1e-05
NEGATIVE = -1e30
ROPE_BASE = 500000.0
MIB = 1 << 20
STEPS = 5
BUNCH = 4
FLIGHT = 3
TURN = 4
LEVEL = 128.0

FREQUENCY = np.exp(np.arange(HD // 2) * (-2.0 * math.log(ROPE_BASE) / HD)).astype(np.float32)

VMEM = pl.BlockSpec(memory_space=pltpu.VMEM)
ANY = pl.BlockSpec(memory_space=pl.ANY)


def own_part():
    return lax.axis_index("tp") % PARTS


def project_kernel(hidden, gain, w, out_ref, hidden_ref, gain_ref, w_ref, normed_ref, hidden_sem, w_sem):
    hidden_copies = [
        pltpu.make_async_copy(hidden, hidden_ref, hidden_sem.at[0]),
        pltpu.make_async_copy(gain, gain_ref, hidden_sem.at[1]),
    ]
    for copy in hidden_copies:
        copy.start()
    w_copies = [
        pltpu.make_async_copy(w.at[:, pl.ds(c * WIDE, WIDE)], w_ref.at[:, pl.ds(c * WIDE, WIDE)], w_sem.at[c])
        for c in range(STEPS)
    ]
    for copy in w_copies[:FLIGHT]:
        copy.start()
    for copy in hidden_copies:
        copy.wait()
    rows = hidden_ref[...].astype(jnp.float32)
    inv = lax.rsqrt(jnp.sum(rows * rows, axis=-1, keepdims=True) / rows.shape[2] + EPSILON)
    at = pl.multiple_of(lax.axis_index("tp") * SHARE, SHARE)
    own = (hidden_ref[:, :, pl.ds(at, SHARE)].astype(jnp.float32) * inv).reshape(ROWS, SHARE)
    normed_ref[...] = (own * gain_ref[...].astype(jnp.float32)[None, :]).astype(jnp.bfloat16)
    for c in range(STEPS):
        w_copies[c].wait()
        if c + FLIGHT < STEPS:
            w_copies[c + FLIGHT].start()
        y = LEVEL * jnp.dot(normed_ref[...], w_ref[:, c * WIDE : (c + 1) * WIDE], preferred_element_type=jnp.float32)
        for u in range(QPK):
            if c < KVH:
                group, chunk = c, u
            else:
                group, chunk = u % KVH, QPK + u // KVH
            for part in range(PARTS):
                out_ref[group * PARTS + part, chunk * 8 : chunk * 8 + 8, :] = y[
                    part * 8 : part * 8 + 8, u * HD : u * HD + HD
                ]


def ask_kernel(lengths_ref, count_ref, other_count_ref, total_ref, ask_ref, new_ref):
    part = own_part()
    me = lax.axis_index("inst")
    total = total_ref[...] * (1.0 / LEVEL)
    counts = count_ref[0, part] + other_count_ref[0, part]
    lengths = lengths_ref[0, pl.ds(part, 1), :]
    row = lax.broadcasted_iota(jnp.int32, (8, N), 0)
    lane = lax.broadcasted_iota(jnp.int32, (8, N), 1)
    terms = jnp.zeros((8, N), jnp.int32)
    for r in range(REQ):
        lent = jnp.broadcast_to(counts[r : r + 1], (8, N)) * BLK
        own = jnp.where(lane == me, jnp.broadcast_to(lengths[:, r : r + 1], (8, N)) + row % POS, 0)
        terms = jnp.where(row // POS == r, lent + own, terms)
    terms = jnp.concatenate([terms.astype(jnp.float32), jnp.zeros((8, HD - N), jnp.float32)], axis=1)
    new_ref[...] = total[64:80]
    tiles = []
    for h in range(QPK):
        ask_ref[0, h * 8 : h * 8 + 8, :] = total[h * 8 : h * 8 + 8]
    for at in range(REQ * POS):
        tiles.append(ask_ref[0, pl.ds(at, QPK, stride=8), :])
    tiles.append(terms)
    whole = jnp.concatenate(tiles, axis=0)
    for i in range(NEAR):
        ask_ref[i] = whole


def rotated(x, cosine, sine):
    return x * cosine + pltpu.roll(x, HD // 2, 1) * sine


def dot_t(a, b):
    return lax.dot_general(a, b, (((1,), (1,)), ((), ())), preferred_element_type=jnp.float32)


def stats_tile(tile, r, columns):
    lane = lax.broadcasted_iota(jnp.int32, (16, HD), 1)
    for k, column in enumerate(columns):
        tile = jnp.where(lane == r * 8 + k, column, tile)
    return tile


def resident_kernel(
    lengths, table, q_ref, new_ref, pool, acc_ref, stat_ref, score_ref, blocks_ref, lengths_ref, table_ref, sem, int_sem
):
    part = own_part()
    copies = [
        pltpu.make_async_copy(table.at[0, part], table_ref, int_sem.at[0]),
        pltpu.make_async_copy(lengths.at[0], lengths_ref, int_sem.at[1]),
    ]
    for copy in copies:
        copy.start()
    for copy in copies:
        copy.wait()
    for r in range(REQ):
        for g in range(0, MAXB, BUNCH):
            used = lengths_ref[part, r] > g * BLK

            @pl.when(used)
            def _():
                for b in range(g, g + BUNCH):
                    at = r * MAXB + b
                    pltpu.make_async_copy(pool.at[table_ref[r, b]], blocks_ref.at[at], sem.at[at // BUNCH]).start()

            @pl.when(jnp.logical_not(used))
            def _():
                at = r * MAXB + g
                blocks_ref[at : at + BUNCH, :, HD:] = jnp.zeros((BUNCH, BLK, HD), jnp.bfloat16)

    new = new_ref[...].astype(jnp.float32)
    pad = jnp.zeros((HD - 8, HD), jnp.float32)
    key_new = jnp.concatenate([new[:8], pad], axis=0).astype(jnp.bfloat16)
    value_new = jnp.concatenate([new[8:], pad], axis=0).astype(jnp.bfloat16)
    lane = lax.broadcasted_iota(jnp.int32, (16, 2 * BLK), 1)
    lane_new = lax.broadcasted_iota(jnp.int32, (16, BLK), 1)
    position = lax.broadcasted_iota(jnp.int32, (16, BLK), 0) // QPK
    tile = jnp.zeros((16, HD), jnp.float32)
    for r in range(REQ):
        query = q_ref[r * 16 : r * 16 + 16, :]
        length = lengths_ref[part, r]
        scores = jnp.where(
            (lane_new >= r * POS) & (lane_new <= r * POS + position), dot_t(query, key_new) * ROOT, NEGATIVE
        )
        score_ref[r, :, MAXB * BLK :] = scores
        top = jnp.max(scores, axis=-1, keepdims=True)
        most = jnp.full((16, 2 * BLK), NEGATIVE, jnp.float32)

        for g in range(0, MAXB, BUNCH):

            @pl.when(length > g * BLK)
            def _():
                at = r * MAXB + g
                here = blocks_ref.at[pl.ds(at, BUNCH)]
                pltpu.make_async_copy(pool.at[pl.ds(0, BUNCH)], here, sem.at[at // BUNCH]).wait()


        def pair(b, first):
            at = r * MAXB + b
            return blocks_ref[at : at + 2, :, first : first + HD].reshape(2 * BLK, HD)

        for b in range(0, MAXB, 2):
            scores = jnp.where(lane + b * BLK < length, dot_t(query, pair(b, 0)) * ROOT, NEGATIVE)
            score_ref[r, :, b * BLK : (b + 2) * BLK] = scores
            most = jnp.maximum(most, scores)
        top = jnp.maximum(top, jnp.max(most, axis=-1, keepdims=True))
        weights = jnp.exp(score_ref[r, :, MAXB * BLK :] - top)
        row_sum = jnp.sum(weights, axis=-1, keepdims=True)
        acc = jnp.dot(weights.astype(jnp.bfloat16), value_new, preferred_element_type=jnp.float32)
        sums = jnp.zeros((16, 2 * BLK), jnp.float32)
        for b in range(0, MAXB, 2):
            weights = jnp.exp(score_ref[r, :, b * BLK : (b + 2) * BLK] - top)
            sums = sums + weights
            acc = acc + jnp.dot(weights.astype(jnp.bfloat16), pair(b, HD), preferred_element_type=jnp.float32)
        row_sum = row_sum + jnp.sum(sums, axis=-1, keepdims=True)
        acc_ref[r * 16 : r * 16 + 16, :] = acc
        tile = stats_tile(tile, r, (top, row_sum))
    stat_ref[...] = tile


def rounded(x):
    return x.astype(jnp.bfloat16).astype(jnp.float32)


def lent_kernel(
    ids,
    counts,
    other_ids,
    other_counts,
    ask_ref,
    new_ref,
    pool_ref,
    other_pool_ref,
    out_ref,
    own_ref,
    own_new_ref,
    q_ref,
    score_ref,
    weight_ref,
    ids_ref,
    count_ref,
    sem,
):
    part = own_part()
    copies = [
        pltpu.make_async_copy(whole.at[0, part], table.at[side], sem.at[at, side])
        for at, (table, both) in enumerate(((ids_ref, (ids, other_ids)), (count_ref, (counts, other_counts))))
        for side, whole in enumerate(both)
    ]
    for copy in copies:
        copy.start()
    me = lax.axis_index("inst")
    core = lax.rem(me, 2)
    pools = (pool_ref, other_pool_ref)

    lane = lax.broadcasted_iota(jnp.int32, (8, HD), 1)
    low = lane < HD // 2
    frequency = jnp.zeros((8, HD), jnp.float32)
    for m in range(HD // 2):
        frequency = jnp.where(lane % (HD // 2) == m, float(FREQUENCY[m]), frequency)
    positions = ask_ref[0, QROWS:ASK, :]
    for k in range(1, NEAR):
        positions = positions + ask_ref[k, QROWS:ASK, :]

    def position(k):
        return jnp.where(core == 0, positions[:, 2 * k : 2 * k + 1], positions[:, 2 * k + 1 : 2 * k + 2])

    for first in range(NEAR // 2):
        second = first + NEAR // 2
        angle = jnp.where(low, position(first), position(second)) * frequency
        cosine, sine = jnp.cos(angle), jnp.sin(angle)
        cosine_turned, sine_turned = pltpu.roll(cosine, HD // 2, 1), pltpu.roll(sine, HD // 2, 1)
        for k, cos, sin in (
            (first, jnp.where(low, cosine, cosine_turned), jnp.where(low, -sine, sine_turned)),
            (second, jnp.where(low, cosine_turned, cosine), jnp.where(low, -sine_turned, sine)),
        ):
            for r in range(REQ):
                both = []
                for at in range(r * POS, r * POS + POS):
                    x = ask_ref[k, at * QPK : at * QPK + QPK, :]
                    both.append(rotated(x, cos[at : at + 1], sin[at : at + 1]))
                q_ref[k, r * 16 : r * 16 + 16, :] = jnp.concatenate(both, axis=0).astype(jnp.bfloat16)
    own_ref[...] = q_ref[me // 2]
    own = jnp.sum(jnp.where(lane == me, positions, 0.0), axis=-1, keepdims=True)
    angle = own * frequency
    sine = jnp.sin(angle)
    key = rotated(new_ref[:8], jnp.cos(angle), jnp.where(low, -sine, sine))
    own_new_ref[...] = jnp.concatenate([key, new_ref[8:]], axis=0).astype(jnp.bfloat16)

    for copy in copies:
        copy.wait()
    lane = lax.broadcasted_iota(jnp.int32, (16, 2 * BLK), 1)

    def valid(n, side):
        return lane < count_ref[side, n % REQ, 2 * (n // REQ) + core] * BLK

    def pair(n, side, first):
        at = 2 * (n // REQ) + core
        halves = [pools[side][ids_ref[side, n % REQ, b, at], :, first : first + HD] for b in range(MCAP)]
        return jnp.concatenate(halves, axis=0)

    for start in range(0, NEAR * REQ, TURN * REQ):
        group = range(start, start + TURN * REQ)
        for n in group:
            query = q_ref[n // REQ, n % REQ * 16 : n % REQ * 16 + 16, :]
            for side in range(2):
                score_ref[n, side] = jnp.where(valid(n, side), dot_t(query, pair(n, side, 0)) * ROOT, NEGATIVE)
        for n in group:
            r = n % REQ
            if r == 0:
                tile = jnp.zeros((16, HD), jnp.float32)
            top = jnp.max(jnp.maximum(score_ref[n, 0], score_ref[n, 1]), axis=-1, keepdims=True)
            row_sum = jnp.zeros((16, 2 * BLK), jnp.float32)
            for side in range(2):
                weights = jnp.where(valid(n, side), jnp.exp(score_ref[n, side] - top), 0.0)
                row_sum = row_sum + weights
                weight_ref[n, side] = weights.astype(jnp.bfloat16)
            row_sum = jnp.sum(row_sum, axis=-1, keepdims=True)
            high = rounded(top)
            middle = rounded(top - high)
            sum_high = rounded(row_sum)
            tile = stats_tile(tile, r, (high, middle, top - high - middle, sum_high, row_sum - sum_high))
            if r == REQ - 1:
                out_ref[n // REQ, 64:80, :] = tile.astype(jnp.bfloat16)
        for n in group:
            acc = jnp.dot(weight_ref[n, 0], pair(n, 0, HD), preferred_element_type=jnp.float32)
            acc = acc + jnp.dot(weight_ref[n, 1], pair(n, 1, HD), preferred_element_type=jnp.float32)
            out_ref[n // REQ, n % REQ * 16 : n % REQ * 16 + 16, :] = acc.astype(jnp.bfloat16)


def combine_kernel(recv_ref, acc_ref, stat_ref, out_ref, total_ref):
    stat = stat_ref[...]
    tops, sums = [], []
    for j in range(NEAR):
        tile = recv_ref[j, 64:80, :].astype(jnp.float32)
        tops.append(tile + pltpu.roll(tile, HD - 1, 1) + pltpu.roll(tile, HD - 2, 1))
        sums.append(pltpu.roll(tile, HD - 3, 1) + pltpu.roll(tile, HD - 4, 1))
    peak = stat
    for j in range(NEAR):
        peak = jnp.maximum(peak, tops[j])
    own = jnp.exp(stat - peak)
    row_sum = own * pltpu.roll(stat, HD - 1, 1)
    scales = []
    for j in range(NEAR):
        scale = jnp.exp(tops[j] - peak)
        row_sum = row_sum + scale * sums[j]
        scales.append(scale)
    for r in range(REQ):
        at = slice(r * 16, r * 16 + 16)

        def spread(tile):
            return jnp.broadcast_to(tile[:, r * 8 : r * 8 + 1], (16, HD))

        acc = spread(own) * acc_ref[at, :]
        for j in range(NEAR):
            acc = acc + spread(scales[j]) * recv_ref[j, at, :].astype(jnp.float32)
        total_ref[at, :] = acc / spread(row_sum)
    for h in range(QPK):
        tile = total_ref[pl.ds(h, 8, stride=QPK), :].astype(jnp.bfloat16)
        for r in range(REQ):
            out_ref[0, 0, r, :, h * HD : (h + 1) * HD] = tile[r * POS : (r + 1) * POS]


def local(hidden, gain, wqkv, pool, lengths, block_table, mig_blocks, mig_count):
    bf16, f32 = jnp.bfloat16, jnp.float32
    shape = jax.ShapeDtypeStruct
    params = pltpu.CompilerParams
    ids = jnp.transpose(mig_blocks, (0, 1, 3, 4, 2))
    counts = jnp.transpose(mig_count, (0, 1, 3, 2))
    blocks = pool[0, 0]
    swap = [(i, i ^ 1) for i in range(N)]
    other_ids = lax.ppermute(ids, "inst", swap)
    other_counts = lax.ppermute(counts, "inst", swap)
    groups = [[i for i in range(N) if i % 2 == core] for core in range(2)]

    partial_value = pl.pallas_call(
        project_kernel,
        in_specs=[ANY, ANY, ANY],
        out_specs=VMEM,
        out_shape=shape((N, MSG, HD), f32),
        scratch_shapes=[
            pltpu.VMEM((PARTS * REQ, POS, N * SHARE), bf16),
            pltpu.VMEM((SHARE,), bf16),
            pltpu.VMEM((SHARE, STEPS * WIDE), bf16),
            pltpu.VMEM((ROWS, SHARE), bf16),
            pltpu.SemaphoreType.DMA((2,)),
            pltpu.SemaphoreType.DMA((STEPS,)),
        ],
        compiler_params=params(vmem_limit_bytes=24 * MIB),
        cost_estimate=pl.CostEstimate(flops=2 * ROWS * SHARE * STEPS * WIDE, bytes_accessed=8 * MIB, transcendentals=ROWS),
        name="project",
    )(*(pltpu.with_memory_space_constraint(x, pltpu.MemorySpace.HBM) for x in (hidden, gain, wqkv)))
    partial_value = partial_value.astype(jnp.float16)
    partial_value, other_ids, other_counts, lent_blocks = lax.optimization_barrier(
        (partial_value, other_ids, other_counts, blocks)
    )
    other_blocks = lax.ppermute(lent_blocks, "inst", swap)
    summands = lax.all_to_all(partial_value, "tp", split_axis=0, concat_axis=0, tiled=True)
    total = jnp.sum(summands.astype(f32), axis=0)
    total, other_blocks = lax.optimization_barrier((total, other_blocks))
    ask, new = pl.pallas_call(
        ask_kernel,
        in_specs=[VMEM, VMEM, VMEM, VMEM],
        out_specs=[VMEM, VMEM],
        out_shape=[shape((NEAR, ASK, HD), f32), shape((16, HD), f32)],
        compiler_params=params(vmem_limit_bytes=16 * MIB),
        name="ask",
    )(lengths, counts, other_counts, total)
    asked = lax.all_to_all(ask, "inst", split_axis=0, concat_axis=0, tiled=True, axis_index_groups=groups)
    answers, queries, new = pl.pallas_call(
        lent_kernel,
        in_specs=[ANY, ANY, ANY, ANY, VMEM, VMEM, VMEM, VMEM],
        out_specs=[VMEM, VMEM, VMEM],
        out_shape=[shape((NEAR, MSG, HD), bf16), shape((QROWS, HD), bf16), shape((16, HD), bf16)],
        scratch_shapes=[
            pltpu.VMEM((NEAR, QROWS, HD), bf16),
            pltpu.VMEM((NEAR * REQ, 2, 16, 2 * BLK), f32),
            pltpu.VMEM((NEAR * REQ, 2, 16, 2 * BLK), bf16),
            pltpu.SMEM((2, REQ, MCAP, N), jnp.int32),
            pltpu.SMEM((2, REQ, N), jnp.int32),
            pltpu.SemaphoreType.DMA((2, 2)),
        ],
        compiler_params=params(vmem_limit_bytes=24 * MIB),
        name="lent",
    )(ids, counts, other_ids, other_counts, asked, new, blocks, other_blocks)
    acc, stat = pl.pallas_call(
        resident_kernel,
        in_specs=[ANY, ANY, VMEM, VMEM, ANY],
        out_specs=[VMEM, VMEM],
        out_shape=[shape((QROWS, HD), f32), shape((16, HD), f32)],
        scratch_shapes=[
            pltpu.VMEM((REQ, 16, (MAXB + 1) * BLK), f32),
            pltpu.VMEM((REQ * MAXB, BLK, 2 * HD), bf16),
            pltpu.SMEM((PARTS, REQ), jnp.int32),
            pltpu.SMEM((REQ, MAXB), jnp.int32),
            pltpu.SemaphoreType.DMA((REQ * MAXB // BUNCH,)),
            pltpu.SemaphoreType.DMA((2,)),
        ],
        compiler_params=params(vmem_limit_bytes=24 * MIB),
        cost_estimate=pl.CostEstimate(flops=100 * MIB * 8, bytes_accessed=16 * MIB, transcendentals=MIB),
        name="resident",
    )(lengths, block_table, queries, new, pltpu.with_memory_space_constraint(blocks, pltpu.MemorySpace.HBM))
    arrived = lax.all_to_all(answers, "inst", split_axis=0, concat_axis=0, tiled=True, axis_index_groups=groups)
    return pl.pallas_call(
        combine_kernel,
        in_specs=[VMEM, VMEM, VMEM],
        out_specs=VMEM,
        out_shape=shape((1, 1, REQ, POS, WIDE), bf16),
        scratch_shapes=[pltpu.VMEM((QROWS, HD), f32)],
        compiler_params=params(vmem_limit_bytes=16 * MIB),
        name="combine",
    )(arrived, acc, stat)


def solution(mesh):
    placed = (
        P("inst", None, None),
        P("tp"),
        P("tp", None),
        P("inst", "tp", None, None, None),
        P("inst", None, None),
        P("inst", None, None, None),
        P("inst", None, None, None, None),
        P("inst", None, None, None),
    )
    return jax.shard_map(
        local,
        mesh=mesh,
        in_specs=placed,
        out_specs=P("inst", "tp", None, None, None),
        check_vma=False,
    )
```
